512 devices in a mesh: group: 8 (over y), fsdp: 8 (over z_lo, core), tp: 8 (over z_hi, x).
Axes of the slice: x: 4, y: 8, z: 8 (z_hi: 2, z_lo: 4; z = z_hi * 4 + z_lo), core: 2. Of those that a mesh axis runs over, the one named last changes fastest.
Arguments:
- hidden_in: bfloat16 [3072, 4, 5120], P(('group', 'fsdp'), None, 'tp'), may hold values from -6 to 6
- norm_gain: bfloat16 [5120], P('tp'), may hold values from 0.099609375 to 1.8984375
- master_query: float32 [5120, 8, 1024], P('fsdp', 'tp', 'group')
- query_gain: float32 [128], replicated, may hold values from 0.1 to 1.9
- kv_cache: bfloat16 [3072, 8, 128, 256], P(('group', 'fsdp'), 'tp'), may hold values from -6 to 6
- lengths: int32 [3072], P(('group', 'fsdp')), may hold values from 4 to 128, as said below
Outputs:
- attended: bfloat16 [3072, 4, 8192], P(('group', 'fsdp'), None, 'tp')
The draws below stay inside these ranges and needn't reach their ends.
Inputs may be any that keep to these rules, and one draw needn't show every extreme that they name: `lengths`: some row has length 128.
All inputs are finite; a program needn't handle non-finite values.
Results may differ from the reference program's by a relative error of at most 0.035.
Values may be sent and summed in bfloat16 or wider, within the bound.
A program may use at most 64 MiB of HBM per device.

```python
import jax
import jax.numpy as jnp
from jax import lax

D = 5120
KVH = 8
HD = 128
BLK = 128
STEPS = 4
CACHE = 128
GQ = 8
BATCH = 3072


def draw_master_query(key, part):
    key = jax.random.fold_in(key, 11)
    base_key, row_key, column_key = jax.random.split(key, 3)
    shape = (D, KVH, GQ * HD)
    base = jax.random.normal(base_key, shape, jnp.float32)
    row_scale = jnp.exp(jax.random.uniform(row_key, (D, 1, 1), jnp.float32, -1.15, 1.15))
    column_scale = jnp.exp(jax.random.uniform(column_key, (1, KVH, GQ * HD), jnp.float32, -1.15, 1.15))
    return (base * row_scale * column_scale * D ** (-0.5)).astype(jnp.float32)


def draw_lengths(key, part):
    key = jax.random.fold_in(key, 23)
    drawn = jax.random.randint(key, (BATCH,), STEPS, CACHE + 1, dtype=jnp.int32)
    return drawn.at[0].set(CACHE)


def block_scale(stream_key, extent, pieces, least, high):
    def one(axis_at, blocks):
        steps = jax.random.uniform(jax.random.fold_in(jax.random.fold_in(stream_key, 6), axis_at), (blocks,), jnp.float32, least / len(pieces), high / len(pieces))
        return jnp.repeat(jnp.exp(steps), extent[axis_at] // blocks).reshape((-1,) + (1,) * (len(extent) - axis_at - 1))

    level = one(*pieces[0])
    for cut in pieces[1:]:
        level = level * one(*cut)
    return level


def gaussian(own_key, extent, deviation, bound, cuts=(), held_as=jnp.bfloat16):
    level = block_scale(own_key, extent, cuts, -0.22, 0.18) if cuts else 1.0
    array = jax.random.normal(own_key, extent, jnp.float32) * deviation * level
    return jnp.minimum(jnp.maximum(array, -bound), bound).astype(held_as)


def setup_inputs(seed: int = 0) -> dict:
    key_list = jax.random.split(jax.random.key(seed), 7)
    return {
        "hidden_in": gaussian(key_list[0], (BATCH, STEPS, D), 1.0, 6.0, ((0, 64), (2, 8))),
        "norm_gain": jnp.clip(1.0 + 0.18 * jax.random.normal(key_list[1], (D,), jnp.float32), 0.099609375, 1.8984375).astype(jnp.bfloat16),
        "master_query": draw_master_query(jax.random.fold_in(key_list[6], 71), 0),
        "query_gain": jnp.clip(1.0 + 0.18 * jax.random.normal(key_list[3], (HD,), jnp.float32), 0.1, 1.9),
        "kv_cache": gaussian(key_list[4], (BATCH, KVH, CACHE, 2 * HD), 1.0, 6.0, ((0, 64), (1, 8))),
        "lengths": draw_lengths(jax.random.fold_in(key_list[6], 71), 0),
    }


epsilon = 1e-06

def quantize(master):
    blocks = master.reshape(D // BLK, BLK, KVH, GQ, HD)
    largest = lax.optimization_barrier(jnp.max(jnp.abs(blocks), axis=(1, 4)))
    scales = ((largest + epsilon) / 127.0).astype(jnp.bfloat16)
    levels = jnp.floor(blocks / scales.astype(jnp.float32)[:, None, :, :, None] + 0.5).astype(jnp.bfloat16)
    return (levels, scales)

def rotate(queries, positions):
    half_width = HD // 2
    frequency = jnp.power(1000000.0, -jnp.arange(half_width, dtype=jnp.float32) * (2.0 / HD))
    angles = positions.astype(jnp.float32)[:, :, None] * frequency[None, None, :]
    cosine = jnp.cos(angles)[:, :, None, None, :]
    sine_part = jnp.sin(angles)[:, :, None, None, :]
    front_half = queries[..., :half_width]
    back_half = queries[..., half_width:]
    return jnp.concatenate([front_half * cosine - back_half * sine_part, back_half * cosine + front_half * sine_part], axis=-1)

def reference(hidden_in, norm_gain, master_query, query_gain, kv_cache, lengths):
    floats = hidden_in.astype(jnp.float32)
    mean_square = lax.optimization_barrier(jnp.mean(floats * floats, axis=-1, keepdims=True))
    normed = (floats * lax.rsqrt(mean_square + epsilon) * norm_gain.astype(jnp.float32)).astype(jnp.bfloat16)
    levels, scales = quantize(master_query)
    token_count = BATCH * STEPS
    token_blocks = normed.reshape(token_count, D // BLK, BLK).transpose(1, 0, 2)

    def add_block(running, element):
        token_rows, level_piece, scale_piece = element
        product = jnp.dot(token_rows, level_piece.reshape(BLK, KVH * GQ * HD), preferred_element_type=jnp.float32)
        product = product.reshape(token_count, KVH, GQ, HD) * scale_piece.astype(jnp.float32)[None, :, :, None]
        return (running + product, None)
    start_sum = jnp.zeros((token_count, KVH, GQ, HD), jnp.float32)
    queries, unused = lax.scan(add_block, start_sum, (token_blocks, levels, scales))
    queries = queries.reshape(BATCH, STEPS, KVH, GQ, HD)
    mean_query = lax.optimization_barrier(jnp.mean(queries * queries, axis=-1, keepdims=True))
    queries = queries * lax.rsqrt(mean_query + epsilon) * query_gain.astype(jnp.float32)
    positions = lengths[:, None] - STEPS + jnp.arange(STEPS, dtype=jnp.int32)[None, :]
    scaled = (rotate(queries, positions) * HD ** (-0.5)).astype(jnp.bfloat16)

    def attend(element):
        query_row, cache_row, position_row = element
        cache_keys = cache_row[..., :HD].astype(jnp.float32)
        cache_values = cache_row[..., HD:].astype(jnp.float32)
        scores = jnp.einsum('skgd,kjd->skgj', query_row.astype(jnp.float32), cache_keys)
        visible = jnp.arange(CACHE, dtype=jnp.int32)[None, None, None, :] <= position_row[:, None, None, None]
        scores = jnp.where(visible, scores, -jnp.inf)
        highest = lax.optimization_barrier(jnp.max(scores, axis=-1, keepdims=True))
        raised = jnp.exp(scores - highest)
        weights = (raised / lax.optimization_barrier(jnp.sum(raised, axis=-1, keepdims=True))).astype(jnp.bfloat16)
        result = jnp.einsum('skgj,kjd->skgd', weights.astype(jnp.float32), cache_values)
        return result.astype(jnp.bfloat16).reshape(STEPS, KVH * GQ * HD)
    return lax.map(attend, (scaled, kv_cache, positions))
```

```python
import functools

import jax
import jax.numpy as jnp
from jax import lax
from jax.experimental import pallas as pl
from jax.experimental.pallas import tpu as pltpu
from jax.sharding import PartitionSpec as P

MESH = pl.DeviceIdType.MESH
HD = 128
BLK = 128
EPS = 1e-06
ROWS = 48
STEPS = 4
TOK = ROWS * STEPS
KB = 640
HEADS = 8
CACHE = 128
F32 = jnp.float32
BF16 = jnp.bfloat16

ORDER = (0, 7, 1, 6, 2, 5, 3, 4)


def remote(src, dst, send_sem, recv_sem, device):
    return pltpu.make_async_remote_copy(
        src_ref=src,
        dst_ref=dst,
        send_sem=send_sem,
        recv_sem=recv_sem,
        device_id=device,
        device_id_type=MESH,
    )


def kernel(
    hid, ssq, master, gain, lens_row, lens, cache, out,
    wown, wbuf, hbuf, ssqb, psend, pkeep, px, zsend, zkeep, qz, qbuf, cacheb, tcos, tsin, rtok,
    cache_sem, w0_send, w_recv, y_send, h0_send, hx_send, h_recv, s_send, s_recv,
    p_send, p_recv, z_send, z_recv,
):
    g, f, t = lax.axis_index("group"), lax.axis_index("fsdp"), lax.axis_index("tp")
    zl, c = f // 2, f % 2
    zh, x = t // 4, t % 4
    half, pair = zl % 2, zl // 2
    up, down = (lax.rem(g + 1, 8), f, t), (lax.rem(g + 7, 8), f, t)
    right = (g, f, zh * 4 + lax.rem(x + 1, 4))
    left = (g, f, zh * 4 + lax.rem(x + 3, 4))
    other = (g, zl * 2 + (1 - c), t)
    partner = (g, (pair * 2 + (1 - half)) * 2 + c, t)
    is_root = c == x % 2
    hid_f = (pair * 2 + zh) * 2 + x % 2
    root_z = is_root & (zh == half)

    cache_copy = pltpu.make_async_copy(cache, cacheb, cache_sem)
    cache_copy.start()

    bar = pltpu.get_barrier_semaphore()

    def tell(device):
        pl.semaphore_signal(bar, inc=1, device_id=device, device_id_type=MESH)

    for device in (up, down, right, left, other, partner):
        tell(device)
    for k in range(1, 8):
        tell((g, f, lax.rem(t + k, 8)))
    for q in range(2):
        src_z = 2 * half + q

        @pl.when(src_z != zl)
        def _():
            tell((g, src_z * 2 + c, t))

    for tb in range(4):
        src_f = pair * 4 + tb

        @pl.when(is_root & jnp.logical_not((src_f == f) & (zh == half)))
        def _():
            tell((g, src_f, half * 4 + x))

    for blk in range(KB // BLK):
        piece = master[blk * BLK:(blk + 1) * BLK, :]
        largest = jnp.max(jnp.abs(piece))
        scale = (jnp.full((1, HD), largest, F32) + EPS) / 127.0
        scale = scale.astype(BF16).astype(F32)
        level = jnp.floor(piece / scale + 0.5)
        wown[blk * BLK:(blk + 1) * BLK, :] = (level * scale).astype(BF16)

    own_q = zl % 2
    own_used = half == pair

    @pl.when(own_used)
    def _():
        wbuf[0, own_q] = wown[...]

    @pl.when(root_z)
    def _():
        hbuf[x // 2, pl.ds((half * 2 + c) * TOK, TOK), :] = hid[...]

    ssqb[t] = ssq[...]

    n_w = jnp.where(own_used, 1, 2)
    n_h = jnp.where((zl == pair * 2 + zh) & is_root, 1, 2)
    pl.semaphore_wait(bar, 6 + 7 + n_w + n_h)

    def w0_copy(i):
        dst_z = pair + 2 * i
        return dst_z != zl, remote(
            wown, wbuf.at[0, own_q], w0_send.at[i], w_recv.at[0, own_q], (g, dst_z * 2 + c, t)
        )

    def h0_copy(i):
        dst_zh = zh if i == 0 else 1 - zh
        same = (i == 0) & (f == hid_f)
        return jnp.logical_not(same), remote(
            hid,
            hbuf.at[x // 2, pl.ds(((zl % 2) * 2 + c) * TOK, TOK), :],
            h0_send.at[i],
            h_recv.at[x // 2, (zl % 2) * 2 + c],
            (g, hid_f, dst_zh * 4 + x),
        )

    def s_copy(k):
        return remote(ssq, ssqb.at[t], s_send.at[k - 1], s_recv.at[t], (g, f, lax.rem(t + k, 8)))

    def y_copy(direction, k, q):
        if direction == 0:
            src, dst, dev = (8 - k) % 8, 7 - k, up
        else:
            src, dst, dev = k, k + 1, down
        return remote(wbuf.at[src, q], wbuf.at[dst, q], y_send.at[direction, k, q], w_recv.at[dst, q], dev)

    def w_wait(slot, q):
        remote(wbuf.at[slot, q], wbuf.at[slot, q], y_send.at[0, 0, 0], w_recv.at[slot, q], up).wait_recv()

    def h_rows(kb, tb):
        return hbuf.at[kb, pl.ds(tb * TOK, TOK), :]

    def h_wait(kb, tb):
        remote(h_rows(kb, tb), h_rows(kb, tb), hx_send.at[0, 0], h_recv.at[kb, tb], right).wait_recv()

    def hx_copy(kb, tb, direction):
        return remote(
            h_rows(kb, tb), h_rows(kb, tb), hx_send.at[direction, tb], h_recv.at[kb, tb],
            right if direction == 0 else left,
        )

    for i in range(2):
        cond, copy = w0_copy(i)

        @pl.when(cond)
        def _():
            copy.start()

    def start_y(k, q):
        if k < 3 or q == 0:
            y_copy(0, k, q).start()
        if k < 3 or q == 1:
            y_copy(1, k, q).start()

    def first(q):
        @pl.when(2 * half + q != zl)
        def _():
            w_wait(0, q)

        start_y(0, q)

    @pl.when(own_used)
    def _():
        start_y(0, own_q)

    for i in range(2):
        cond, copy = h0_copy(i)

        @pl.when(cond)
        def _():
            copy.start()

    for k in range(1, 8):
        s_copy(k).start()

    kb_root = x // 2
    kb_left = lax.rem(x + 3, 4) // 2
    kb_right = lax.rem(x + 1, 4) // 2

    def h_step(i):
        @pl.when(is_root)
        def _():
            tb = i

            @pl.when(jnp.logical_not(root_z & (half * 2 + c == tb)))
            def _():
                h_wait(kb_root, tb)

            hx_copy(kb_root, tb, 0).start()
            hx_copy(kb_root, tb, 1).start()

        @pl.when(jnp.logical_not(is_root))
        def _():
            if i % 2 == 0:
                tb = i // 2
                h_wait(kb_left, tb)
                hx_copy(kb_left, tb, 0).start()
            else:
                tb = 2 + i // 2
                h_wait(kb_right, tb)
                hx_copy(kb_right, tb, 1).start()

    def first_other(q):
        @pl.when(jnp.logical_not(own_used & (own_q == q)))
        def _():
            w_wait(0, q)
            start_y(0, q)

    def w_step(k, q):
        w_wait(8 - k, q)
        if k < 3 or q == 0:
            y_copy(0, k, q).start()
        w_wait(k, q)
        if k < 3 or q == 1:
            y_copy(1, k, q).start()

    first_other(0)
    first_other(1)

    eye = lax.broadcasted_iota(jnp.int32, (ROWS, ROWS), 0) == lax.broadcasted_iota(jnp.int32, (ROWS, ROWS), 1)
    column = jnp.sum(jnp.where(eye, lens_row[...].astype(F32), 0.0), axis=1, keepdims=True)
    lane = lax.broadcasted_iota(jnp.int32, (1, HD), 1)
    frequency = jnp.exp((lane % 64).astype(F32) * F32(-2.0 / HD * 13.815510557964274))
    sign = jnp.where(lane < 64, -1.0, 1.0).astype(F32)
    gain_row = gain[...] * F32(HD ** -0.5)
    gain_far = pltpu.roll(jnp.broadcast_to(gain_row, (8, HD)), 64, 1)[0:1, :] * sign
    for s in range(STEPS):
        angle = (column + F32(s - STEPS)) * frequency
        tcos[s * ROWS:(s + 1) * ROWS, :] = jnp.cos(angle) * gain_row
        tsin[s * ROWS:(s + 1) * ROWS, :] = jnp.sin(angle) * gain_far

    h_step(0)
    w_step(1, 0)
    h_step(1)
    w_step(1, 1)
    h_step(2)
    w_step(2, 0)
    h_step(3)
    w_step(2, 1)

    for k in range(1, 8):
        tt = lax.rem(t + k, 8)
        remote(ssqb.at[tt], ssqb.at[tt], s_send.at[0], s_recv.at[tt], right).wait_recv()
    total = jnp.sum(ssqb[...], axis=0)
    wide = lax.broadcasted_iota(jnp.int32, (HD, HD), 0) == lax.broadcasted_iota(jnp.int32, (HD, HD), 1)
    col0 = jnp.sum(jnp.where(wide, total[0:1, :], 0.0), axis=1, keepdims=True)
    col1 = jnp.sum(jnp.where(wide, total[1:2, :], 0.0), axis=1, keepdims=True)
    rtok[0:HD, :] = jnp.broadcast_to(lax.rsqrt(col0 * F32(1.0 / 5120) + EPS), (HD, HD))
    rtok[HD:TOK, :] = jnp.broadcast_to(lax.rsqrt(col1 * F32(1.0 / 5120) + EPS), (HD, HD))[0:TOK - HD]

    @pl.when(is_root)
    def _():
        far = lax.rem(x + 2, 4) // 2
        for tb in range(4):
            h_wait(far, tb)

    @pl.when(jnp.logical_not(is_root))
    def _():
        h_wait(kb_left, 2)
        h_wait(kb_left, 3)
        h_wait(kb_right, 0)
        h_wait(kb_right, 1)

    def p_copy(d):
        return remote(psend.at[d], px.at[d], p_send.at[d], p_recv.at[d], other)

    def z_copy(d):
        return remote(zsend.at[d], qz.at[d], z_send.at[d], z_recv.at[d], partner)

    def multiply(d):
        w0 = wbuf[d, 0]
        w1 = wbuf[d, 1]
        for z in range(2):
            for cc in range(2):
                rows = (z * 2 + cc) * TOK
                part = jnp.dot(hbuf[0, rows:rows + TOK, :], w0, preferred_element_type=F32)
                part += jnp.dot(hbuf[1, rows:rows + TOK, :], w1, preferred_element_type=F32)

                @pl.when(c == cc)
                def _():
                    pkeep[d, z] = part

                @pl.when(c != cc)
                def _():
                    psend[d, z] = part.astype(BF16)

        p_copy(d).start()

    def second(d):
        p_copy(d).wait_recv()
        zkeep[d] = pkeep[d, half] + px[d, half].astype(F32)
        zsend[d] = (pkeep[d, 1 - half] + px[d, 1 - half].astype(F32)).astype(BF16)
        z_copy(d).start()

    def third(d):
        z_copy(d).wait_recv()
        head = lax.rem(g + d, 8)
        query = (zkeep[d] + qz[d].astype(F32)) * rtok[...]
        mean = jnp.mean(query * query, axis=1, keepdims=True)
        query = query * lax.rsqrt(mean + EPS)
        turned = query * tcos[...] + pltpu.roll(query, 64, 1) * tsin[...]
        for s in range(STEPS):
            qbuf[pl.ds(head * STEPS + s, ROWS, stride=HEADS * STEPS), :] = turned[s * ROWS:(s + 1) * ROWS, :]

    for i in range(HEADS + 4):
        if i < HEADS:
            d = ORDER[i]
            if i == 3:
                w_step(3, 0)
                w_step(3, 1)
            if d == 4:
                w_wait(4, 0)
                w_wait(4, 1)
            multiply(d)
        if 0 <= i - 2 < HEADS:
            second(ORDER[i - 2])
        if 0 <= i - 4 < HEADS:
            third(ORDER[i - 4])

    cache_copy.wait()
    unroll = 4
    slot = lax.broadcasted_iota(jnp.int32, (HEADS * STEPS, CACHE), 1)
    step = lax.broadcasted_iota(jnp.int32, (HEADS * STEPS, CACHE), 0) % STEPS

    def rows_of(i, carry):
        for u in range(unroll):
            b = i * unroll + u
            query = qbuf[pl.ds(pl.multiple_of(b * HEADS * STEPS, HEADS * STEPS), HEADS * STEPS), :].astype(BF16)
            scores = lax.dot_general(
                query, cacheb[b, :, 0:HD], (((1,), (1,)), ((), ())), preferred_element_type=F32
            )
            scores = jnp.where(slot <= step + (lens[b] - STEPS), scores, -jnp.inf)
            raised = jnp.exp(scores - jnp.max(scores, axis=1, keepdims=True))
            total = jnp.sum(raised, axis=1, keepdims=True)
            result = jnp.dot(raised.astype(BF16), cacheb[b, :, HD:], preferred_element_type=F32)
            out[b] = (result / total).astype(BF16)
        return carry

    lax.fori_loop(0, ROWS // unroll, rows_of, 0)

    for i in range(2):
        for cond, copy in (w0_copy(i), h0_copy(i)):

            @pl.when(cond)
            def _():
                copy.wait_send()

    for k in range(1, 8):
        s_copy(k).wait_send()
    for k in range(4):
        for q in range(2):
            if k < 3 or q == 0:
                y_copy(0, k, q).wait_send()
            if k < 3 or q == 1:
                y_copy(1, k, q).wait_send()
    for tb in range(4):
        @pl.when(is_root)
        def _():
            hx_copy(kb_root, tb, 0).wait_send()
            hx_copy(kb_root, tb, 1).wait_send()

        @pl.when(jnp.logical_not(is_root))
        def _():
            if tb < 2:
                hx_copy(kb_left, tb, 0).wait_send()
            else:
                hx_copy(kb_right, tb, 1).wait_send()
    for d in range(HEADS):
        p_copy(d).wait_send()
        z_copy(d).wait_send()


def shards(hidden_in, norm_gain, master_query, query_gain, kv_cache, lengths):
    floats = hidden_in.astype(F32)
    squares = jnp.sum(floats * floats, axis=-1).T.reshape(1, TOK)
    squares = jnp.pad(squares, ((0, 0), (0, 8 * HD - TOK))).reshape(8, HD)
    gained = (floats * norm_gain.astype(F32)).astype(BF16)
    gained = gained.transpose(1, 0, 2).reshape(TOK, KB)
    vmem = pl.BlockSpec(memory_space=pltpu.VMEM)
    dma = pltpu.SemaphoreType.DMA
    call = pl.pallas_call(
        kernel,
        out_shape=jax.ShapeDtypeStruct((ROWS, HEADS * STEPS, HD), BF16),
        in_specs=[vmem, vmem, vmem, vmem, vmem, pl.BlockSpec(memory_space=pltpu.SMEM), pl.BlockSpec(memory_space=pl.ANY)],
        out_specs=vmem,
        scratch_shapes=[
            pltpu.VMEM((KB, HD), BF16),
            pltpu.VMEM((HEADS, 2, KB, HD), BF16),
            pltpu.VMEM((2, 4 * TOK, KB), BF16),
            pltpu.VMEM((8, 8, HD), F32),
            pltpu.VMEM((HEADS, 2, TOK, HD), BF16),
            pltpu.VMEM((HEADS, 2, TOK, HD), F32),
            pltpu.VMEM((HEADS, 2, TOK, HD), BF16),
            pltpu.VMEM((HEADS, TOK, HD), BF16),
            pltpu.VMEM((HEADS, TOK, HD), F32),
            pltpu.VMEM((HEADS, TOK, HD), BF16),
            pltpu.VMEM((ROWS * HEADS * STEPS, HD), F32),
            pltpu.VMEM((ROWS, CACHE, 2 * HD), BF16),
            pltpu.VMEM((TOK, HD), F32),
            pltpu.VMEM((TOK, HD), F32),
            pltpu.VMEM((TOK, HD), F32),
            dma,
            dma((2,)),
            dma((HEADS, 2)),
            dma((2, 4, 2)),
            dma((2,)),
            dma((2, 4)),
            dma((2, 4)),
            dma((7,)),
            dma((8,)),
            dma((HEADS,)),
            dma((HEADS,)),
            dma((HEADS,)),
            dma((HEADS,)),
        ],
        compiler_params=pltpu.CompilerParams(
            collective_id=0, has_side_effects=True, vmem_limit_bytes=48 << 20
        ),
    )
    result = call(
        gained,
        squares,
        master_query.reshape(KB, HD),
        query_gain.reshape(1, HD),
        lengths.reshape(1, ROWS),
        lengths,
        kv_cache.reshape(ROWS, CACHE, 2 * HD),
    )
    return result.reshape(ROWS, HEADS, STEPS, HD).transpose(0, 2, 1, 3).reshape(ROWS, STEPS, HEADS * HD)


def solution(mesh):
    in_specs = (
        P(("group", "fsdp"), None, "tp"),
        P("tp"),
        P("fsdp", "tp", "group"),
        P(),
        P(("group", "fsdp"), "tp", None, None),
        P(("group", "fsdp")),
    )
    out_specs = P(("group", "fsdp"), None, "tp")
    return jax.shard_map(shards, mesh=mesh, in_specs=in_specs, out_specs=out_specs, check_vma=False)
```

```python
import functools

import jax
import jax.numpy as jnp
from jax import lax
from jax.experimental import pallas as pl
from jax.experimental.pallas import tpu as pltpu
from jax.sharding import PartitionSpec as P

MESH = pl.DeviceIdType.MESH
HD = 128
BLK = 128
EPS = 1e-06
ROWS = 48
STEPS = 4
TOK = ROWS * STEPS
KB = 640
HEADS = 8
CACHE = 128
WSUB = 2
WROWS = KB // WSUB
F32 = jnp.float32
BF16 = jnp.bfloat16

GROUPS = ((0,), (7, 1), (6, 2), (5, 3), (4,))


def remote(src, dst, send_sem, recv_sem, device):
    return pltpu.make_async_remote_copy(
        src_ref=src,
        dst_ref=dst,
        send_sem=send_sem,
        recv_sem=recv_sem,
        device_id=device,
        device_id_type=MESH,
    )


def kernel(
    hid_in, gain_in, master_in, qgain_in, lens_in, cache, out,
    hidv, hidf, hid, gain, master, qgain, lens, cacheb,
    wown, wbuf, hbuf, ssqb, psend, pkeep, px, zsend, zkeep, qz, qbuf, tcos, tsin, rtok, last,
    in_sem, w0_send, w_recv, y_send, h0_send, hx_send, h_recv, s_send, s_recv,
    p_send, p_recv, z_send, z_recv,
):
    g, f, t = lax.axis_index("group"), lax.axis_index("fsdp"), lax.axis_index("tp")
    zl, c = f // 2, f % 2
    zh, x = t // 4, t % 4
    side, pair = zl % 2, zl // 2
    half = (side + zh + pair + 1) % 2
    up, down = (lax.rem(g + 1, 8), f, t), (lax.rem(g + 7, 8), f, t)
    right = (g, f, zh * 4 + lax.rem(x + 1, 4))
    left = (g, f, zh * 4 + lax.rem(x + 3, 4))
    other = (g, zl * 2 + (1 - c), t)
    partner = (g, (pair * 2 + (1 - side)) * 2 + c, t)
    is_root = c == x % 2
    root_z = is_root & (zh == half)
    own_tb = side * 2 + c
    own_q = zl % 2
    own_used = half == pair

    inputs = [
        pltpu.make_async_copy(src, dst, in_sem.at[i])
        for i, (src, dst) in enumerate(
            ((master_in, master), (hid_in, hidv), (gain_in, gain), (qgain_in, qgain), (lens_in, lens), (cache, cacheb))
        )
    ]
    for copy in inputs:
        copy.start()

    bar = pltpu.get_barrier_semaphore()

    def tell(device):
        pl.semaphore_signal(bar, inc=1, device_id=device, device_id_type=MESH)

    for q in range(2):
        src_z = 2 * half + q

        @pl.when(src_z != zl)
        def _():
            tell((g, src_z * 2 + c, t))

    for tb in range(4):
        src_f = pair * 4 + tb

        @pl.when(is_root & jnp.logical_not((src_f == f) & (zh == half)))
        def _():
            tell((g, src_f, half * 4 + x))

    for device in (up, down, right, left, other, partner):
        tell(device)
    for k in range(1, 8):
        tell((g, f, lax.rem(t + k, 8)))

    inputs[0].wait()
    for blk in range(KB // BLK):
        piece = master[blk * BLK:(blk + 1) * BLK, :]
        largest = jnp.max(jnp.abs(piece))
        scale = (jnp.full((1, HD), largest, F32) + EPS) / 127.0
        scale = scale.astype(BF16).astype(F32)
        level = jnp.floor(piece / scale + 0.5)
        wown[blk * BLK:(blk + 1) * BLK, :] = (level * scale).astype(BF16)

    @pl.when(own_used)
    def _():
        wbuf[0, own_q] = wown[...]

    n_w = jnp.where(own_used, 1, 2)
    n_h = jnp.where((side != pair) & is_root, 1, 2)
    pl.semaphore_wait(bar, 6 + 7 + n_w + n_h)

    def w0_copy(i, hs):
        dst_z = 2 * i + lax.rem(pair + zh + 1 + i, 2)
        rows = pl.ds(hs * WROWS, WROWS)
        return dst_z != zl, remote(
            wown.at[rows, :], wbuf.at[0, own_q, rows, :], w0_send.at[i, hs], w_recv.at[0, own_q, hs],
            (g, dst_z * 2 + c, t),
        )

    def h0_copy(i, sub):
        dst_side = (1 - pair) if i == 0 else pair
        dst_f = (pair * 2 + dst_side) * 2 + x % 2
        dst_zh = zh if i == 0 else 1 - zh
        needed = jnp.logical_not((side != pair) & is_root) if i == 0 else jnp.bool_(True)
        return needed, remote(
            hid.at[pl.ds(sub * ROWS, ROWS), :],
            hbuf.at[x // 2, sub, pl.ds(own_tb * ROWS, ROWS), :],
            h0_send.at[i, sub],
            h_recv.at[x // 2, own_tb, sub],
            (g, dst_f, dst_zh * 4 + x),
        )

    def s_copy(k):
        return remote(ssqb.at[t], ssqb.at[t], s_send.at[k - 1], s_recv.at[t], (g, f, lax.rem(t + k, 8)))

    def w_rows(slot, q, hs):
        return wbuf.at[slot, q, pl.ds(hs * WROWS, WROWS), :]

    def y_copy(direction, k, q, hs):
        if direction == 0:
            src, dst, dev = (8 - k) % 8, 7 - k, up
        else:
            src, dst, dev = k, k + 1, down
        return remote(
            w_rows(src, q, hs), w_rows(dst, q, hs), y_send.at[direction, k, q, hs], w_recv.at[dst, q, hs], dev
        )

    def w_wait(slot, q, hs):
        rows = w_rows(slot, q, hs)
        remote(rows, rows, y_send.at[0, 0, 0, 0], w_recv.at[slot, q, hs], up).wait_recv()

    def h_rows(kb, tb, sub):
        return hbuf.at[kb, sub, pl.ds(tb * ROWS, ROWS), :]

    def h_wait(kb, tb, sub):
        rows = h_rows(kb, tb, sub)
        remote(rows, rows, hx_send.at[0, 0, 0], h_recv.at[kb, tb, sub], right).wait_recv()

    def hx_copy(kb, tb, sub, direction):
        rows = h_rows(kb, tb, sub)
        return remote(
            rows, rows, hx_send.at[direction, tb, sub], h_recv.at[kb, tb, sub], right if direction == 0 else left
        )

    def start_y(k, q, hs):
        if k < 3 or q == 0:
            y_copy(0, k, q, hs).start()
        if k < 3 or q == 1:
            y_copy(1, k, q, hs).start()

    for i in (1 - pair, pair):
        for hs in range(WSUB):
            cond, copy = w0_copy(i, hs)

            @pl.when(cond)
            def _():
                copy.start()

    @pl.when(own_used)
    def _():
        for hs in range(WSUB):
            start_y(0, own_q, hs)

    inputs[1].wait()
    inputs[2].wait()
    eye = lax.broadcasted_iota(jnp.int32, (ROWS, HD), 0) == lax.broadcasted_iota(jnp.int32, (ROWS, HD), 1)
    for kt in range(KB // HD):
        hidf[kt * TOK:(kt + 1) * TOK, :] = hidv[:, :, kt * HD:(kt + 1) * HD].astype(F32).reshape(TOK, HD)
    gains = gain[...].astype(F32).reshape(1, KB)
    ssq_rows = []
    for s in range(STEPS):
        squares = jnp.zeros((ROWS, HD), F32)
        for kt in range(KB // HD):
            piece = hidf[pl.ds(kt * TOK + s, ROWS, stride=STEPS), :]
            squares += piece * piece
            hid[s * ROWS:(s + 1) * ROWS, kt * HD:(kt + 1) * HD] = (piece * gains[:, kt * HD:(kt + 1) * HD]).astype(BF16)
        ssq_rows.append(
            jnp.sum(jnp.where(eye, jnp.sum(squares, axis=1, keepdims=True), 0.0), axis=0, keepdims=True)
        )
    ssqb[t] = jnp.concatenate(ssq_rows + [jnp.zeros((8 - STEPS, HD), F32)], axis=0)

    for sub in range(STEPS):
        for i in (1, 0):
            cond, copy = h0_copy(i, sub)

            @pl.when(cond)
            def _():
                copy.start()

    for k in range(1, 8):
        s_copy(k).start()

    @pl.when(root_z)
    def _():
        for sub in range(STEPS):
            hbuf[x // 2, sub, pl.ds(own_tb * ROWS, ROWS), :] = hid[sub * ROWS:(sub + 1) * ROWS, :]

    kb_root = x // 2
    kb_left = lax.rem(x + 3, 4) // 2
    kb_right = lax.rem(x + 1, 4) // 2

    def h_step(sub):
        @pl.when(is_root)
        def _():
            for tb in range(4):
                @pl.when(jnp.logical_not(root_z & (own_tb == tb)))
                def _():
                    h_wait(kb_root, tb, sub)

                hx_copy(kb_root, tb, sub, 0).start()
                hx_copy(kb_root, tb, sub, 1).start()

        @pl.when(jnp.logical_not(is_root))
        def _():
            for tb in range(2):
                h_wait(kb_left, tb, sub)
                hx_copy(kb_left, tb, sub, 0).start()
                h_wait(kb_right, tb + 2, sub)
                hx_copy(kb_right, tb + 2, sub, 1).start()

    def h_last(sub):
        @pl.when(is_root)
        def _():
            far = lax.rem(x + 2, 4) // 2
            for tb in range(4):
                h_wait(far, tb, sub)

        @pl.when(jnp.logical_not(is_root))
        def _():
            for tb in range(2):
                h_wait(kb_left, tb + 2, sub)
                h_wait(kb_right, tb, sub)

    def first_other(hs):
        for q in range(2):
            @pl.when(jnp.logical_not(own_used & (own_q == q)))
            def _():
                w_wait(0, q, hs)
                start_y(0, q, hs)

    def w_step(k, q):
        for hs in range(WSUB):
            w_wait(8 - k, q, hs)
            if k < 3 or q == 0:
                y_copy(0, k, q, hs).start()
            w_wait(k, q, hs)
            if k < 3 or q == 1:
                y_copy(1, k, q, hs).start()

    for hs in range(WSUB):
        first_other(hs)

    inputs[3].wait()
    inputs[4].wait()
    lens_row = lens[...].astype(F32).reshape(1, ROWS)
    lens_wide = jnp.concatenate([lens_row, jnp.zeros((1, HD - ROWS), F32)], axis=1)
    column = jnp.sum(jnp.where(eye, lens_wide, 0.0), axis=1, keepdims=True)
    lane = lax.broadcasted_iota(jnp.int32, (1, HD), 1)
    frequency = jnp.exp((lane % 64).astype(F32) * F32(-2.0 / HD * 13.815510557964274))
    sign = jnp.where(lane < 64, -1.0, 1.0).astype(F32)
    gain_row = qgain[...].reshape(1, HD) * F32(HD ** -0.5)
    gain_far = pltpu.roll(jnp.broadcast_to(gain_row, (8, HD)), 64, 1)[0:1, :] * sign
    for s in range(STEPS):
        angle = (column + F32(s - STEPS)) * frequency
        tcos[s * ROWS:(s + 1) * ROWS, :] = jnp.cos(angle) * gain_row
        tsin[s * ROWS:(s + 1) * ROWS, :] = jnp.sin(angle) * gain_far
    row_at = lax.broadcasted_iota(jnp.int32, (ROWS, HD), 0)
    lane_at = lax.broadcasted_iota(jnp.int32, (ROWS, HD), 1)
    for i in range(ROWS // 4):
        chosen = jnp.sum(jnp.where(row_at == 4 * i + lane_at // 32, column, 0.0), axis=0, keepdims=True)
        last[i] = jnp.broadcast_to(chosen + (lane % STEPS - STEPS).astype(F32), (8, HD))

    h_step(0)
    w_step(1, 0)
    h_step(1)
    h_step(2)
    w_step(1, 1)
    h_step(3)
    w_step(2, 0)
    w_step(2, 1)

    for k in range(1, 8):
        tt = lax.rem(t + k, 8)
        remote(ssqb.at[tt], ssqb.at[tt], s_send.at[0], s_recv.at[tt], right).wait_recv()
    total = jnp.sum(ssqb[...], axis=0)
    for s in range(STEPS):
        mean = jnp.sum(jnp.where(eye, total[s:s + 1, :], 0.0), axis=1, keepdims=True) * F32(1.0 / 5120)
        rtok[s * ROWS:(s + 1) * ROWS, :] = jnp.broadcast_to(lax.rsqrt(mean + EPS), (ROWS, HD))

    def p_copy(sub, n):
        lanes = pl.ds(0, HD * len(GROUPS[n]))
        return remote(
            psend.at[sub, n, :, :, lanes], px.at[sub, n, :, :, lanes], p_send.at[sub, n], p_recv.at[sub, n], other
        )

    def z_copy(sub, n):
        lanes = pl.ds(0, HD * len(GROUPS[n]))
        return remote(
            zsend.at[sub, n, :, lanes], qz.at[sub, n, :, lanes], z_send.at[sub, n], z_recv.at[sub, n], partner
        )

    def multiply(sub, n):
        width = HD * len(GROUPS[n])
        weights = jnp.concatenate(
            [jnp.concatenate([wbuf[d, 0], wbuf[d, 1]], axis=0) for d in GROUPS[n]], axis=1
        )
        tokens = jnp.concatenate([hbuf[0, sub], hbuf[1, sub]], axis=1)
        part = jnp.dot(tokens, weights, preferred_element_type=F32)
        for z in range(2):
            for cc in range(2):
                piece = part[(z * 2 + cc) * ROWS:(z * 2 + cc + 1) * ROWS, :]

                @pl.when(c == cc)
                def _():
                    pkeep[sub, n, z, :, 0:width] = piece

                @pl.when(c != cc)
                def _():
                    psend[sub, n, z, :, 0:width] = piece.astype(BF16)

        p_copy(sub, n).start()

    def second(sub, n):
        width = HD * len(GROUPS[n])
        p_copy(sub, n).wait_recv()
        zkeep[sub, n, :, 0:width] = pkeep[sub, n, side, :, 0:width] + px[sub, n, side, :, 0:width].astype(F32)
        zsend[sub, n, :, 0:width] = (
            pkeep[sub, n, 1 - side, :, 0:width] + px[sub, n, 1 - side, :, 0:width].astype(F32)
        ).astype(BF16)
        z_copy(sub, n).start()

    def third(sub, n):
        z_copy(sub, n).wait_recv()
        rows = slice(sub * ROWS, (sub + 1) * ROWS)
        for m, d in enumerate(GROUPS[n]):
            lanes = slice(m * HD, (m + 1) * HD)
            head = lax.rem(g + d, 8)
            query = (zkeep[sub, n, :, lanes] + qz[sub, n, :, lanes].astype(F32)) * rtok[rows, :]
            mean = jnp.mean(query * query, axis=1, keepdims=True)
            query = query * lax.rsqrt(mean + EPS)
            turned = query * tcos[rows, :] + pltpu.roll(query, 64, 1) * tsin[rows, :]
            qbuf[pl.ds(head * STEPS + sub, ROWS, stride=HEADS * STEPS), :] = turned

    def each(stage, sub, ns):
        for n in ns:
            stage(sub, n)

    h_last(0)
    each(multiply, 0, (0, 1, 2))
    w_step(3, 0)
    h_last(1)
    each(multiply, 1, (0, 1, 2))
    each(second, 0, (0, 1, 2))
    w_step(3, 1)
    h_last(2)
    each(multiply, 2, (0, 1, 2, 3))
    each(second, 1, (0, 1, 2))
    each(third, 0, (0, 1, 2))
    multiply(0, 3)
    multiply(1, 3)
    h_last(3)
    each(multiply, 3, (0, 1, 2, 3))
    each(second, 2, (0, 1, 2, 3))
    second(0, 3)
    second(1, 3)
    each(third, 1, (0, 1, 2))
    for hs in range(WSUB):
        w_wait(4, 0, hs)
        w_wait(4, 1, hs)
    for sub in range(STEPS):
        multiply(sub, 4)
    each(second, 3, (0, 1, 2, 3))
    each(third, 2, (0, 1, 2, 3))
    for sub in range(STEPS):
        second(sub, 4)
    third(0, 3)
    third(1, 3)
    each(third, 3, (0, 1, 2, 3))
    for sub in range(STEPS):
        third(sub, 4)

    inputs[5].wait()
    key_at = lax.broadcasted_iota(jnp.int32, (CACHE, HD), 0).astype(F32)
    lane_row = lax.broadcasted_iota(jnp.int32, (CACHE, HD), 1) // 32

    def four_rows(i, carry):
        base = pl.multiple_of(i * 128, 128)
        queries = jnp.transpose(qbuf[pl.ds(base, 128), :]).astype(BF16)
        scores = jnp.zeros((CACHE, HD), F32)
        for r in range(4):
            one = jnp.dot(cacheb[i * 4 + r, :, 0:HD], queries, preferred_element_type=F32)
            scores = one if r == 0 else jnp.where(lane_row == r, one, scores)
        scores = jnp.where(key_at <= last[i, 0:1, :], scores, -jnp.inf)
        raised = jnp.exp(scores - jnp.max(scores, axis=0, keepdims=True))
        weights = raised * (1.0 / jnp.sum(raised, axis=0, keepdims=True))
        weights = jnp.transpose(weights).astype(BF16)
        for r in range(4):
            result = jnp.dot(weights[r * 32:(r + 1) * 32, :], cacheb[i * 4 + r, :, HD:], preferred_element_type=F32)
            out[i * 4 + r] = result.astype(BF16)
        return carry

    lax.fori_loop(0, ROWS // 4, four_rows, 0, unroll=2)

    for i in range(2):
        for hs in range(WSUB):
            cond, copy = w0_copy(i, hs)

            @pl.when(cond)
            def _():
                copy.wait_send()

        for sub in range(STEPS):
            cond, copy = h0_copy(i, sub)

            @pl.when(cond)
            def _():
                copy.wait_send()

    for k in range(1, 8):
        s_copy(k).wait_send()
    for k in range(4):
        for q in range(2):
            for hs in range(WSUB):
                if k < 3 or q == 0:
                    y_copy(0, k, q, hs).wait_send()
                if k < 3 or q == 1:
                    y_copy(1, k, q, hs).wait_send()
    for sub in range(STEPS):
        @pl.when(is_root)
        def _():
            for tb in range(4):
                hx_copy(kb_root, tb, sub, 0).wait_send()
                hx_copy(kb_root, tb, sub, 1).wait_send()

        @pl.when(jnp.logical_not(is_root))
        def _():
            for tb in range(2):
                hx_copy(kb_left, tb, sub, 0).wait_send()
                hx_copy(kb_right, tb + 2, sub, 1).wait_send()

    for sub in range(STEPS):
        for n in range(len(GROUPS)):
            p_copy(sub, n).wait_send()
            z_copy(sub, n).wait_send()


def shards(hidden_in, norm_gain, master_query, query_gain, kv_cache, lengths):
    dma = pltpu.SemaphoreType.DMA
    call = pl.pallas_call(
        kernel,
        out_shape=jax.ShapeDtypeStruct((ROWS, HEADS * STEPS, HD), BF16),
        in_specs=[pl.BlockSpec(memory_space=pltpu.HBM)] * 6,
        out_specs=pl.BlockSpec(memory_space=pltpu.VMEM),
        scratch_shapes=[
            pltpu.VMEM((ROWS, STEPS, KB), BF16),
            pltpu.VMEM((KB // HD * TOK, HD), F32),
            pltpu.VMEM((TOK, KB), BF16),
            pltpu.VMEM((KB,), BF16),
            pltpu.VMEM((KB, HD), F32),
            pltpu.VMEM((HD,), F32),
            pltpu.VMEM((ROWS,), jnp.int32),
            pltpu.VMEM((ROWS, CACHE, 2 * HD), BF16),
            pltpu.VMEM((KB, HD), BF16),
            pltpu.VMEM((HEADS, 2, KB, HD), BF16),
            pltpu.VMEM((2, STEPS, 4 * ROWS, KB), BF16),
            pltpu.VMEM((8, 8, HD), F32),
            pltpu.VMEM((STEPS, len(GROUPS), 2, ROWS, 2 * HD), BF16),
            pltpu.VMEM((STEPS, len(GROUPS), 2, ROWS, 2 * HD), F32),
            pltpu.VMEM((STEPS, len(GROUPS), 2, ROWS, 2 * HD), BF16),
            pltpu.VMEM((STEPS, len(GROUPS), ROWS, 2 * HD), BF16),
            pltpu.VMEM((STEPS, len(GROUPS), ROWS, 2 * HD), F32),
            pltpu.VMEM((STEPS, len(GROUPS), ROWS, 2 * HD), BF16),
            pltpu.VMEM((ROWS * HEADS * STEPS, HD), F32),
            pltpu.VMEM((TOK, HD), F32),
            pltpu.VMEM((TOK, HD), F32),
            pltpu.VMEM((TOK, HD), F32),
            pltpu.VMEM((ROWS // 4, 8, HD), F32),
            dma((6,)),
            dma((2, WSUB)),
            dma((HEADS, 2, WSUB)),
            dma((2, 4, 2, WSUB)),
            dma((2, STEPS)),
            dma((2, 4, STEPS)),
            dma((2, 4, STEPS)),
            dma((7,)),
            dma((8,)),
            dma((STEPS, len(GROUPS))),
            dma((STEPS, len(GROUPS))),
            dma((STEPS, len(GROUPS))),
            dma((STEPS, len(GROUPS))),
        ],
        compiler_params=pltpu.CompilerParams(
            collective_id=0, has_side_effects=True, vmem_limit_bytes=62 << 20
        ),
    )
    result = call(
        hidden_in,
        norm_gain,
        master_query.reshape(KB, HD),
        query_gain,
        lengths,
        kv_cache.reshape(ROWS, CACHE, 2 * HD),
    )
    return result.reshape(ROWS, HEADS, STEPS, HD).transpose(0, 2, 1, 3).reshape(ROWS, STEPS, HEADS * HD)


def solution(mesh):
    in_specs = (
        P(("group", "fsdp"), None, "tp"),
        P("tp"),
        P("fsdp", "tp", "group"),
        P(),
        P(("group", "fsdp"), "tp", None, None),
        P(("group", "fsdp")),
    )
    out_specs = P(("group", "fsdp"), None, "tp")
    return jax.shard_map(shards, mesh=mesh, in_specs=in_specs, out_specs=out_specs, check_vma=False)
```

```python
import functools

import jax
import jax.numpy as jnp
from jax import lax
from jax.experimental import pallas as pl
from jax.experimental.pallas import tpu as pltpu
from jax.sharding import PartitionSpec as P

MESH = pl.DeviceIdType.MESH
HD = 128
BLK = 128
EPS = 1e-06
ROWS = 48
STEPS = 4
TOK = ROWS * STEPS
KB = 640
HEADS = 8
CACHE = 128
SUBS = 4
LATE = 2
SUB = TOK // SUBS
PIECES = ((0, 3), (6, 2), (3, 3), (8, 2))
F32 = jnp.float32
BF16 = jnp.bfloat16

GROUPS = ((0, 7, 1), (6, 2), (5, 3))
WIDE = 3 * HD


def remote(src, dst, send_sem, recv_sem, device):
    return pltpu.make_async_remote_copy(
        src_ref=src,
        dst_ref=dst,
        send_sem=send_sem,
        recv_sem=recv_sem,
        device_id=device,
        device_id_type=MESH,
    )


def kernel(
    hid_in, gain_in, master_in, qgain_in, lens_in, cache, out,
    hidv, hidf, hid, gain, master, qgain, lens, cacheb,
    wown, wbuf, hbuf, ssqb, psend, pkeep, px, zsend, zkeep, qz,
    psend4, pkeep4, px4, zsend4, zkeep4, qz4, qbuf, tcos, tsin, rtok, last,
    in_sem, w0_send, w_recv, y_send, h0_send, hx_send, hz_recv, hx_recv, s_send, s_recv,
    p_send, p_recv, z_send, z_recv, last_sem,
):
    g, f, t = lax.axis_index("group"), lax.axis_index("fsdp"), lax.axis_index("tp")
    zl, c = f // 2, f % 2
    zh, x = t // 4, t % 4
    side, pair = zl % 2, zl // 2
    up, down = (lax.rem(g + 1, 8), f, t), (lax.rem(g + 7, 8), f, t)
    right = (g, f, zh * 4 + lax.rem(x + 1, 4))
    left = (g, f, zh * 4 + lax.rem(x + 3, 4))
    other = (g, zl * 2 + (1 - c), t)
    partner = (g, (pair * 2 + (1 - side)) * 2 + c, t)
    is_root = c == x % 2
    own_tb = side * 2 + c
    inputs = [
        pltpu.make_async_copy(src, dst, in_sem.at[i])
        for i, (src, dst) in enumerate(
            ((master_in, master), (hid_in, hidv), (gain_in, gain), (qgain_in, qgain), (lens_in, lens), (cache, cacheb))
        )
    ]
    for copy in inputs:
        copy.start()

    def z_at(k):
        k_pair, k_side = k // 2, k % 2
        return (g, (lax.rem(pair + k_pair, 2) * 2 + lax.rem(side + k_side, 2)) * 2 + c, t)

    bar = pltpu.get_barrier_semaphore()

    def tell(device):
        pl.semaphore_signal(bar, inc=1, device_id=device, device_id_type=MESH)

    for k in range(1, 4):
        tell(z_at(k))

    for src_zh in range(2):
        for tb in range(4):
            src_f = pair * 4 + tb

            @pl.when(is_root & jnp.logical_not((src_f == f) & (zh == src_zh)))
            def _():
                tell((g, src_f, src_zh * 4 + x))

    for device in (up, down, right, left, other, partner):
        tell(device)
    for k in range(1, 8):
        tell((g, f, lax.rem(t + k, 8)))

    inputs[0].wait()
    for blk in range(KB // BLK):
        piece = master[blk * BLK:(blk + 1) * BLK, :]
        largest = jnp.max(jnp.abs(piece), axis=(0, 1), keepdims=True)
        scale = (largest + EPS) / 127.0
        scale = scale.astype(BF16).astype(F32)
        level = jnp.floor(piece / scale + 0.5)
        wown[blk * BLK:(blk + 1) * BLK, :] = (level * scale).astype(BF16)

    wbuf[0, 0:3 * HD, :] = wown[0:3 * HD, :]

    pl.semaphore_wait(bar, 3 + 6 + 7 + jnp.where(is_root, 3, 4))

    def w0_copy(k):
        first, tiles = PIECES[k]
        start = 0 if tiles == 3 else 3
        return remote(
            wown.at[pl.ds(start * HD, tiles * HD), :], w_rows(0, k), w0_send.at[k - 1], w_recv.at[0, k], z_at(k)
        )

    def h0_copy(match, plane, sub):
        tiles, start = (3, 0) if match == 0 else (2, 3)
        dst_side = lax.rem(x // 2 + match, 2)
        dst_f = (pair * 2 + dst_side) * 2 + x % 2
        rel = lax.rem(zh + pair, 2)
        same = is_root & (side == dst_side) if plane == 0 else jnp.bool_(False)
        first = rel * tiles + (0 if match == 0 else 6)
        return jnp.logical_not(same), first, remote(
            hid.at[pl.ds(start, tiles), pl.ds(sub * SUB, SUB), :],
            hbuf.at[pl.ds(first, tiles), sub, pl.ds(own_tb * SUB, SUB), :],
            h0_send.at[match, plane, sub],
            hz_recv.at[rel, own_tb, sub],
            (g, dst_f, (zh if plane == 0 else 1 - zh) * 4 + x),
        )

    def s_copy(k):
        return remote(ssqb.at[t], ssqb.at[t], s_send.at[k - 1], s_recv.at[t], (g, f, lax.rem(t + k, 8)))

    def w_rows(slot, p):
        first, tiles = PIECES[p]
        return wbuf.at[slot, pl.ds(first * HD, tiles * HD), :]

    def y_copy(direction, k, p):
        if direction == 0:
            src, dst, dev = (8 - k) % 8, 7 - k, up
        else:
            src, dst, dev = k, k + 1, down
        return remote(w_rows(src, p), w_rows(dst, p), y_send.at[direction, k, p], w_recv.at[dst, p], dev)

    def y_goes(direction, k, p):
        return k < 3 or p // 2 == direction

    def w_wait(slot, p):
        rows = w_rows(slot, p)
        remote(rows, rows, y_send.at[0, 0, 0], w_recv.at[slot, p], up).wait_recv()

    def hz_wait(match, rel, tb, sub):
        tiles = 3 if match == 0 else 2
        rows = hbuf.at[pl.ds((0 if match == 0 else 6) + rel * tiles, tiles), sub, pl.ds(tb * SUB, SUB), :]
        remote(rows, rows, hx_send.at[0, 0, 0], hz_recv.at[rel, tb, sub], right).wait_recv()

    def h_rows(match, tp, sub):
        tiles = pl.ds(0, 6) if match == 0 else pl.ds(6, 4)
        return hbuf.at[tiles, sub, pl.ds(tp * 2 * SUB, 2 * SUB), :]

    def h_wait(match, tp, sub):
        rows = h_rows(match, tp, sub)
        remote(rows, rows, hx_send.at[0, 0, 0], hx_recv.at[match, tp, sub], right).wait_recv()

    def hx_copy(match, tp, sub, direction):
        rows = h_rows(match, tp, sub)
        return remote(
            rows, rows, hx_send.at[direction, tp, sub], hx_recv.at[match, tp, sub],
            right if direction == 0 else left,
        )

    def start_y(k, p):
        for direction in range(2):
            if y_goes(direction, k, p):
                y_copy(direction, k, p).start()

    start_y(0, 0)
    w0_copy(1).start()

    inputs[1].wait()
    inputs[2].wait()
    eye = lax.broadcasted_iota(jnp.int32, (ROWS, HD), 0) == lax.broadcasted_iota(jnp.int32, (ROWS, HD), 1)
    for kt in range(KB // HD):
        hidf[kt * TOK:(kt + 1) * TOK, :] = hidv[:, :, kt * HD:(kt + 1) * HD].astype(F32).reshape(TOK, HD)
    gains = gain[...].astype(F32).reshape(1, KB)
    ssq_rows = []
    for s in range(STEPS):
        squares = jnp.zeros((ROWS, HD), F32)
        for kt in range(KB // HD):
            piece = hidf[pl.ds(kt * TOK + s, ROWS, stride=STEPS), :]
            squares += piece * piece
            hid[kt, s * ROWS:(s + 1) * ROWS, :] = (piece * gains[:, kt * HD:(kt + 1) * HD]).astype(BF16)
        ssq_rows.append(
            jnp.sum(jnp.where(eye, jnp.sum(squares, axis=1, keepdims=True), 0.0), axis=0, keepdims=True)
        )
    ssqb[t] = jnp.concatenate(ssq_rows + [jnp.zeros((8 - STEPS, HD), F32)], axis=0)

    for sub in range(SUBS):
        if sub == LATE:
            w0_copy(2).start()
            w0_copy(3).start()
        for plane in (1, 0):
            for match in range(2):
                cond, first, copy = h0_copy(match, plane, sub)

                @pl.when(cond)
                def _():
                    copy.start()

    if LATE == SUBS:
        w0_copy(2).start()
        w0_copy(3).start()
    for k in range(1, 8):
        s_copy(k).start()

    rel_own = lax.rem(zh + pair, 2)
    for match in range(2):
        tiles, start = (3, 0) if match == 0 else (2, 3)

        @pl.when(is_root & (side == lax.rem(x // 2 + match, 2)))
        def _():
            for sub in range(SUBS):
                for kt in range(tiles):
                    hbuf[rel_own * tiles + (0 if match == 0 else 6) + kt, sub, pl.ds(own_tb * SUB, SUB), :] = hid[
                        start + kt, sub * SUB:(sub + 1) * SUB, :
                    ]

    root_match = x // 2 == side
    left_match = lax.rem(x + 3, 4) // 2 == side

    def for_match(flag, body):
        @pl.when(flag)
        def _():
            body(0)

        @pl.when(jnp.logical_not(flag))
        def _():
            body(1)

    def h_step(sub):
        @pl.when(is_root)
        def _():
            def root(match):
                for tp in range(2):
                    for tb in (2 * tp, 2 * tp + 1):
                        for rel in range(2):
                            @pl.when(jnp.logical_not((rel_own == rel) & (own_tb == tb)))
                            def _():
                                hz_wait(match, rel, tb, sub)

                    hx_copy(match, tp, sub, 0).start()
                    hx_copy(match, tp, sub, 1).start()

            for_match(root_match, root)

        @pl.when(jnp.logical_not(is_root))
        def _():
            def passer(match):
                h_wait(match, 0, sub)
                hx_copy(match, 0, sub, 0).start()
                h_wait(1 - match, 1, sub)
                hx_copy(1 - match, 1, sub, 1).start()

            for_match(left_match, passer)

    def h_last(sub):
        @pl.when(is_root)
        def _():
            def root(match):
                for tp in range(2):
                    h_wait(1 - match, tp, sub)

            for_match(root_match, root)

        @pl.when(jnp.logical_not(is_root))
        def _():
            def passer(match):
                h_wait(match, 1, sub)
                h_wait(1 - match, 0, sub)

            for_match(left_match, passer)

    def w_step(k, p):
        w_wait(8 - k, p)
        if y_goes(0, k, p):
            y_copy(0, k, p).start()
        w_wait(k, p)
        if y_goes(1, k, p):
            y_copy(1, k, p).start()

    def w_first(p):
        w_wait(0, p)
        start_y(0, p)

    w_first(1)

    inputs[3].wait()
    inputs[4].wait()
    lens_row = lens[...].astype(F32).reshape(1, ROWS)
    lens_wide = jnp.concatenate([lens_row, jnp.zeros((1, HD - ROWS), F32)], axis=1)
    column = jnp.sum(jnp.where(eye, lens_wide, 0.0), axis=1, keepdims=True)
    lane = lax.broadcasted_iota(jnp.int32, (1, HD), 1)
    frequency = jnp.exp((lane % 64).astype(F32) * F32(-2.0 / HD * 13.815510557964274))
    sign = jnp.where(lane < 64, -1.0, 1.0).astype(F32)
    gain_row = qgain[...].reshape(1, HD) * F32(HD ** -0.5)
    gain_far = pltpu.roll(jnp.broadcast_to(gain_row, (8, HD)), 64, 1)[0:1, :] * sign
    for s in range(STEPS):
        angle = (column + F32(s - STEPS)) * frequency
        tcos[s * ROWS:(s + 1) * ROWS, :] = jnp.cos(angle) * gain_row
        tsin[s * ROWS:(s + 1) * ROWS, :] = jnp.sin(angle) * gain_far
    row_at = lax.broadcasted_iota(jnp.int32, (ROWS, HD), 0)
    lane_at = lax.broadcasted_iota(jnp.int32, (ROWS, HD), 1)
    for i in range(ROWS // 4):
        chosen = jnp.sum(jnp.where(row_at == 4 * i + lane_at // 32, column, 0.0), axis=0, keepdims=True)
        last[i] = jnp.broadcast_to(chosen + (lane % STEPS - STEPS).astype(F32), (8, HD))

    w_step(1, 0)
    w_step(1, 1)
    h_step(0)
    w_step(2, 0)
    w_step(2, 1)
    h_step(1)
    w_first(2)
    w_first(3)
    w_step(3, 0)
    w_step(3, 1)
    h_step(2)
    w_step(1, 2)
    w_step(1, 3)
    h_step(3)

    for k in range(1, 8):
        tt = lax.rem(t + k, 8)
        remote(ssqb.at[tt], ssqb.at[tt], s_send.at[0], s_recv.at[tt], right).wait_recv()
    total = jnp.sum(ssqb[...], axis=0)
    for s in range(STEPS):
        mean = jnp.sum(jnp.where(eye, total[s:s + 1, :], 0.0), axis=1, keepdims=True) * F32(1.0 / 5120)
        rtok[s * ROWS:(s + 1) * ROWS, :] = jnp.broadcast_to(lax.rsqrt(mean + EPS), (ROWS, HD))

    def p_copy(u, n):
        lanes = pl.ds(0, HD * len(GROUPS[n]))
        return remote(
            psend.at[u, n, :, :, lanes], px.at[u, n, :, :, lanes], p_send.at[u, n], p_recv.at[u, n], other
        )

    def z_copy(u, n):
        lanes = pl.ds(0, HD * len(GROUPS[n]))
        return remote(
            zsend.at[u, n, :, lanes], qz.at[u, n, :, lanes], z_send.at[u, n], z_recv.at[u, n], partner
        )

    def tokens_of(subs):
        return jnp.concatenate(
            [jnp.concatenate([hbuf[kt, sub] for kt in range(2 * KB // HD)], axis=1) for sub in subs], axis=0
        )

    def subs_of(u):
        return range(u * SUBS // 2, (u + 1) * SUBS // 2)

    def split(part, m, z):
        first_core = part[(m * 4 + z * 2) * SUB:(m * 4 + z * 2 + 1) * SUB, :]
        second_core = part[(m * 4 + z * 2 + 1) * SUB:(m * 4 + z * 2 + 2) * SUB, :]
        return jnp.where(c == 0, first_core, second_core), jnp.where(c == 0, second_core, first_core).astype(BF16)

    def multiply(u, n):
        width = HD * len(GROUPS[n])
        weights = jnp.concatenate([wbuf[d] for d in GROUPS[n]], axis=1)
        part = jnp.dot(tokens_of(subs_of(u)), weights, preferred_element_type=F32)
        for m in range(SUBS // 2):
            for z in range(2):
                keep, send = split(part, m, z)
                pkeep[u, n, z, m * SUB:(m + 1) * SUB, 0:width] = keep
                psend[u, n, z, m * SUB:(m + 1) * SUB, 0:width] = send
        p_copy(u, n).start()

    def second(u, n):
        width = HD * len(GROUPS[n])
        p_copy(u, n).wait_recv()
        zkeep[u, n, :, 0:width] = pkeep[u, n, side, :, 0:width] + px[u, n, side, :, 0:width].astype(F32)
        zsend[u, n, :, 0:width] = (
            pkeep[u, n, 1 - side, :, 0:width] + px[u, n, 1 - side, :, 0:width].astype(F32)
        ).astype(BF16)
        z_copy(u, n).start()

    def finish(queries, rows):
        means = [jnp.mean(query * query, axis=1, keepdims=True) for query in queries]
        queries = [query * lax.rsqrt(mean + EPS) for query, mean in zip(queries, means)]
        cosines, sines = tcos[rows, :], tsin[rows, :]
        return [query * cosines + pltpu.roll(query, 64, 1) * sines for query in queries]

    def third(u):
        rows = slice(u * 2 * ROWS, (u + 1) * 2 * ROWS)
        slots, queries = [], []
        for n in range(len(GROUPS)):
            z_copy(u, n).wait_recv()
        factors = rtok[rows, :]
        for n in range(len(GROUPS)):
            for m, d in enumerate(GROUPS[n]):
                lanes = slice(m * HD, (m + 1) * HD)
                slots.append(d)
                queries.append((zkeep[u, n, :, lanes] + qz[u, n, :, lanes].astype(F32)) * factors)
        for d, turned in zip(slots, finish(queries, rows)):
            head = lax.rem(g + d, 8)
            for m in range(2):
                qbuf[pl.ds(head * STEPS + 2 * u + m, ROWS, stride=HEADS * STEPS), :] = turned[m * ROWS:(m + 1) * ROWS, :]

    def p4_copy():
        return remote(psend4, px4, last_sem.at[0], last_sem.at[1], other)

    def z4_copy():
        return remote(zsend4, qz4, last_sem.at[2], last_sem.at[3], partner)

    def multiply4():
        part = jnp.dot(tokens_of(range(SUBS)), wbuf[4], preferred_element_type=F32)
        for sub in range(SUBS):
            rows = slice(sub * SUB, (sub + 1) * SUB)
            for z in range(2):
                pkeep4[z, rows, :], psend4[z, rows, :] = split(part, sub, z)
        p4_copy().start()

    def second4():
        p4_copy().wait_recv()
        zkeep4[...] = pkeep4[side] + px4[side].astype(F32)
        zsend4[...] = (pkeep4[1 - side] + px4[1 - side].astype(F32)).astype(BF16)
        z4_copy().start()

    def third4():
        z4_copy().wait_recv()
        head = lax.rem(g + 4, 8)
        query = (zkeep4[...] + qz4[...].astype(F32)) * rtok[...]
        turned = finish([query], slice(0, TOK))[0]
        for sub in range(STEPS):
            qbuf[pl.ds(head * STEPS + sub, ROWS, stride=HEADS * STEPS), :] = turned[sub * ROWS:(sub + 1) * ROWS, :]

    def early_sent():
        for k in (1, 2, 3):
            w0_copy(k).wait_send()
        for sub in range(SUBS):
            for plane in range(2):
                for match in range(2):
                    cond, first, copy = h0_copy(match, plane, sub)

                    @pl.when(cond)
                    def _():
                        copy.wait_send()

        for k in range(1, 8):
            s_copy(k).wait_send()
        for k in range(3):
            for p in range(4):
                y_copy(0, k, p).wait_send()
                y_copy(1, k, p).wait_send()
        for sub in range(SUBS):
            @pl.when(is_root)
            def _():
                def root(match):
                    for tp in range(2):
                        hx_copy(match, tp, sub, 0).wait_send()
                        hx_copy(match, tp, sub, 1).wait_send()

                for_match(root_match, root)

            @pl.when(jnp.logical_not(is_root))
            def _():
                def passer(match):
                    hx_copy(match, 0, sub, 0).wait_send()
                    hx_copy(1 - match, 1, sub, 1).wait_send()

                for_match(left_match, passer)

    h_last(0)
    w_step(2, 2)
    w_step(2, 3)
    h_last(1)
    multiply(0, 0)
    multiply(0, 1)
    w_step(3, 2)
    w_step(3, 3)
    second(0, 0)
    second(0, 1)
    h_last(2)
    multiply(0, 2)
    h_last(3)
    multiply(1, 0)
    multiply(1, 1)
    multiply(1, 2)
    second(0, 2)
    early_sent()
    for p in range(4):
        w_wait(4, p)
    multiply4()
    second(1, 0)
    second(1, 1)
    second(1, 2)
    second4()
    third(0)
    third(1)
    third4()

    inputs[5].wait()
    key_at = lax.broadcasted_iota(jnp.int32, (CACHE, HD), 0).astype(F32)
    lane_row = lax.broadcasted_iota(jnp.int32, (CACHE, HD), 1) // 32

    def four_rows(i, carry):
        base = pl.multiple_of(i * 128, 128)
        queries = jnp.transpose(qbuf[pl.ds(base, 128), :]).astype(BF16)
        scores = jnp.zeros((CACHE, HD), F32)
        for r in range(4):
            one = jnp.dot(cacheb[i * 4 + r, :, 0:HD], queries, preferred_element_type=F32)
            scores = one if r == 0 else jnp.where(lane_row == r, one, scores)
        scores = jnp.where(key_at <= last[i, 0:1, :], scores, -jnp.inf)
        raised = jnp.exp(scores - jnp.max(scores, axis=0, keepdims=True))
        weights = raised * (1.0 / jnp.sum(raised, axis=0, keepdims=True))
        weights = jnp.transpose(weights).astype(BF16)
        for r in range(4):
            result = jnp.dot(weights[r * 32:(r + 1) * 32, :], cacheb[i * 4 + r, :, HD:], preferred_element_type=F32)
            out[i * 4 + r] = result.astype(BF16)
        return carry

    lax.fori_loop(0, ROWS // 4, four_rows, 0, unroll=6)

    for p in range(4):
        y_copy(p // 2, 3, p).wait_send()
    for u in range(2):
        for n in range(len(GROUPS)):
            p_copy(u, n).wait_send()
            z_copy(u, n).wait_send()
    p4_copy().wait_send()
    z4_copy().wait_send()


def shards(hidden_in, norm_gain, master_query, query_gain, kv_cache, lengths):
    dma = pltpu.SemaphoreType.DMA
    call = pl.pallas_call(
        kernel,
        out_shape=jax.ShapeDtypeStruct((ROWS, HEADS * STEPS, HD), BF16),
        in_specs=[pl.BlockSpec(memory_space=pltpu.HBM)] * 6,
        out_specs=pl.BlockSpec(memory_space=pltpu.VMEM),
        scratch_shapes=[
            pltpu.VMEM((ROWS, STEPS, KB), BF16),
            pltpu.VMEM((KB // HD * TOK, HD), F32),
            pltpu.VMEM((KB // HD, TOK, HD), BF16),
            pltpu.VMEM((KB,), BF16),
            pltpu.VMEM((KB, HD), F32),
            pltpu.VMEM((HD,), F32),
            pltpu.VMEM((ROWS,), jnp.int32),
            pltpu.VMEM((ROWS, CACHE, 2 * HD), BF16),
            pltpu.VMEM((KB, HD), BF16),
            pltpu.VMEM((HEADS, 2 * KB, HD), BF16),
            pltpu.VMEM((2 * KB // HD, SUBS, 4 * SUB, HD), BF16),
            pltpu.VMEM((8, 8, HD), F32),
            pltpu.VMEM((2, len(GROUPS), 2, 2 * ROWS, WIDE), BF16),
            pltpu.VMEM((2, len(GROUPS), 2, 2 * ROWS, WIDE), F32),
            pltpu.VMEM((2, len(GROUPS), 2, 2 * ROWS, WIDE), BF16),
            pltpu.VMEM((2, len(GROUPS), 2 * ROWS, WIDE), BF16),
            pltpu.VMEM((2, len(GROUPS), 2 * ROWS, WIDE), F32),
            pltpu.VMEM((2, len(GROUPS), 2 * ROWS, WIDE), BF16),
            pltpu.VMEM((2, TOK, HD), BF16),
            pltpu.VMEM((2, TOK, HD), F32),
            pltpu.VMEM((2, TOK, HD), BF16),
            pltpu.VMEM((TOK, HD), BF16),
            pltpu.VMEM((TOK, HD), F32),
            pltpu.VMEM((TOK, HD), BF16),
            pltpu.VMEM((ROWS * HEADS * STEPS, HD), F32),
            pltpu.VMEM((TOK, HD), F32),
            pltpu.VMEM((TOK, HD), F32),
            pltpu.VMEM((TOK, HD), F32),
            pltpu.VMEM((ROWS // 4, 8, HD), F32),
            dma((6,)),
            dma((3,)),
            dma((HEADS, 4)),
            dma((2, 4, 4)),
            dma((2, 2, SUBS)),
            dma((2, 2, SUBS)),
            dma((2, 4, SUBS)),
            dma((2, 2, SUBS)),
            dma((7,)),
            dma((8,)),
            dma((2, len(GROUPS))),
            dma((2, len(GROUPS))),
            dma((2, len(GROUPS))),
            dma((2, len(GROUPS))),
            dma((4,)),
        ],
        compiler_params=pltpu.CompilerParams(
            collective_id=0, has_side_effects=True, vmem_limit_bytes=62 << 20
        ),
    )
    result = call(
        hidden_in,
        norm_gain,
        master_query.reshape(KB, HD),
        query_gain,
        lengths,
        kv_cache.reshape(ROWS, CACHE, 2 * HD),
    )
    return result.reshape(ROWS, HEADS, STEPS, HD).transpose(0, 2, 1, 3).reshape(ROWS, STEPS, HEADS * HD)


def solution(mesh):
    in_specs = (
        P(("group", "fsdp"), None, "tp"),
        P("tp"),
        P("fsdp", "tp", "group"),
        P(),
        P(("group", "fsdp"), "tp", None, None),
        P(("group", "fsdp")),
    )
    out_specs = P(("group", "fsdp"), None, "tp")
    return jax.shard_map(shards, mesh=mesh, in_specs=in_specs, out_specs=out_specs, check_vma=False)
```

```python
import functools

import jax
import jax.numpy as jnp
from jax import lax
from jax.experimental import pallas as pl
from jax.experimental.pallas import tpu as pltpu
from jax.sharding import PartitionSpec as P

MESH = pl.DeviceIdType.MESH
HD = 128
BLK = 128
EPS = 1e-06
ROWS = 48
STEPS = 4
TOK = ROWS * STEPS
KB = 640
HEADS = 8
CACHE = 128
SUBS = 4
LATE = 2
SUB = TOK // SUBS
PIECES = ((0, 3), (6, 2), (3, 3), (8, 2))
F32 = jnp.float32
BF16 = jnp.bfloat16

GROUPS = ((0, 7, 1), (6, 2), (5, 3))
WIDE = 3 * HD


def remote(src, dst, send_sem, recv_sem, device):
    return pltpu.make_async_remote_copy(
        src_ref=src,
        dst_ref=dst,
        send_sem=send_sem,
        recv_sem=recv_sem,
        device_id=device,
        device_id_type=MESH,
    )


def kernel(
    hid_in, gain_in, master_in, qgain_in, lens_in, cache, out,
    hidv, hidf, hid, gain, master, qgain, lens, cacheb,
    wown, wbuf, hbuf, ssqb, psend, pkeep, px, zsend, zkeep, qz,
    psend4, pkeep4, px4, zsend4, zkeep4, qz4, qbuf, tcos, tsin, rtok, last,
    in_sem, w0_send, w_recv, y_send, h0_send, hx_send, hz_recv, hx_recv, s_send, s_recv,
    p_send, p_recv, z_send, z_recv, last_sem,
):
    g, f, t = lax.axis_index("group"), lax.axis_index("fsdp"), lax.axis_index("tp")
    zl, c = f // 2, f % 2
    zh, x = t // 4, t % 4
    side, pair = zl % 2, zl // 2
    up, down = (lax.rem(g + 1, 8), f, t), (lax.rem(g + 7, 8), f, t)
    right = (g, f, zh * 4 + lax.rem(x + 1, 4))
    left = (g, f, zh * 4 + lax.rem(x + 3, 4))
    other = (g, zl * 2 + (1 - c), t)
    partner = (g, (pair * 2 + (1 - side)) * 2 + c, t)
    is_root = c == x % 2
    own_tb = side * 2 + c
    inputs = [
        pltpu.make_async_copy(src, dst, in_sem.at[i])
        for i, (src, dst) in enumerate(
            ((master_in, master), (hid_in, hidv), (gain_in, gain), (qgain_in, qgain), (lens_in, lens), (cache, cacheb))
        )
    ]
    for copy in inputs:
        copy.start()

    def z_at(k):
        k_pair, k_side = k // 2, k % 2
        return (g, (lax.rem(pair + k_pair, 2) * 2 + lax.rem(side + k_side, 2)) * 2 + c, t)

    bar = pltpu.get_barrier_semaphore()

    def tell(device):
        pl.semaphore_signal(bar, inc=1, device_id=device, device_id_type=MESH)

    for k in range(1, 4):
        tell(z_at(k))

    for src_zh in range(2):
        for tb in range(4):
            src_f = pair * 4 + tb

            @pl.when(is_root & jnp.logical_not((src_f == f) & (zh == src_zh)))
            def _():
                tell((g, src_f, src_zh * 4 + x))

    for device in (up, down, right, left, other, partner):
        tell(device)
    for k in range(1, 8):
        tell((g, f, lax.rem(t + k, 8)))

    inputs[0].wait()
    for blk in range(KB // BLK):
        piece = master[blk * BLK:(blk + 1) * BLK, :]
        largest = jnp.max(jnp.abs(piece), axis=(0, 1), keepdims=True)
        scale = (largest + EPS) / 127.0
        scale = scale.astype(BF16).astype(F32)
        level = jnp.floor(piece / scale + 0.5)
        wown[blk * BLK:(blk + 1) * BLK, :] = (level * scale).astype(BF16)

    wbuf[0, 0:3 * HD, :] = wown[0:3 * HD, :]

    inputs[1].wait()
    inputs[2].wait()
    eye = lax.broadcasted_iota(jnp.int32, (ROWS, HD), 0) == lax.broadcasted_iota(jnp.int32, (ROWS, HD), 1)
    for kt in range(KB // HD):
        hidf[kt * TOK:(kt + 1) * TOK, :] = hidv[:, :, kt * HD:(kt + 1) * HD].astype(F32).reshape(TOK, HD)
    gains = gain[...].astype(F32).reshape(1, KB)
    ssq_rows = []
    for s in range(STEPS):
        squares = jnp.zeros((ROWS, HD), F32)
        for kt in range(KB // HD):
            piece = hidf[pl.ds(kt * TOK + s, ROWS, stride=STEPS), :]
            squares += piece * piece
            hid[kt, s * ROWS:(s + 1) * ROWS, :] = (piece * gains[:, kt * HD:(kt + 1) * HD]).astype(BF16)
        ssq_rows.append(
            jnp.sum(jnp.where(eye, jnp.sum(squares, axis=1, keepdims=True), 0.0), axis=0, keepdims=True)
        )
    ssqb[t] = jnp.concatenate(ssq_rows + [jnp.zeros((8 - STEPS, HD), F32)], axis=0)

    inputs[3].wait()
    inputs[4].wait()
    lens_row = lens[...].astype(F32).reshape(1, ROWS)
    lens_wide = jnp.concatenate([lens_row, jnp.zeros((1, HD - ROWS), F32)], axis=1)
    column = jnp.sum(jnp.where(eye, lens_wide, 0.0), axis=1, keepdims=True)
    lane = lax.broadcasted_iota(jnp.int32, (1, HD), 1)
    frequency = jnp.exp((lane % 64).astype(F32) * F32(-2.0 / HD * 13.815510557964274))
    sign = jnp.where(lane < 64, -1.0, 1.0).astype(F32)
    gain_row = qgain[...].reshape(1, HD) * F32(HD ** -0.5)
    gain_far = pltpu.roll(jnp.broadcast_to(gain_row, (8, HD)), 64, 1)[0:1, :] * sign
    for s in range(STEPS):
        angle = (column + F32(s - STEPS)) * frequency
        tcos[s * ROWS:(s + 1) * ROWS, :] = jnp.cos(angle) * gain_row
        tsin[s * ROWS:(s + 1) * ROWS, :] = jnp.sin(angle) * gain_far
    row_at = lax.broadcasted_iota(jnp.int32, (ROWS, HD), 0)
    lane_at = lax.broadcasted_iota(jnp.int32, (ROWS, HD), 1)
    for i in range(ROWS // 4):
        chosen = jnp.sum(jnp.where(row_at == 4 * i + lane_at // 32, column, 0.0), axis=0, keepdims=True)
        last[i] = jnp.broadcast_to(chosen + (lane % STEPS - STEPS).astype(F32), (8, HD))

    pl.semaphore_wait(bar, 3 + 6 + 7 + jnp.where(is_root, 3, 4))

    def w0_copy(k):
        first, tiles = PIECES[k]
        start = 0 if tiles == 3 else 3
        return remote(
            wown.at[pl.ds(start * HD, tiles * HD), :], w_rows(0, k), w0_send.at[k - 1], w_recv.at[0, k], z_at(k)
        )

    def h0_copy(match, plane, sub):
        tiles, start = (3, 0) if match == 0 else (2, 3)
        dst_side = lax.rem(x // 2 + match, 2)
        dst_f = (pair * 2 + dst_side) * 2 + x % 2
        rel = lax.rem(zh + pair, 2)
        same = is_root & (side == dst_side) if plane == 0 else jnp.bool_(False)
        first = rel * tiles + (0 if match == 0 else 6)
        return jnp.logical_not(same), first, remote(
            hid.at[pl.ds(start, tiles), pl.ds(sub * SUB, SUB), :],
            hbuf.at[pl.ds(first, tiles), sub, pl.ds(own_tb * SUB, SUB), :],
            h0_send.at[match, plane, sub],
            hz_recv.at[rel, own_tb, sub],
            (g, dst_f, (zh if plane == 0 else 1 - zh) * 4 + x),
        )

    def s_copy(k):
        return remote(ssqb.at[t], ssqb.at[t], s_send.at[k - 1], s_recv.at[t], (g, f, lax.rem(t + k, 8)))

    def w_rows(slot, p):
        first, tiles = PIECES[p]
        return wbuf.at[slot, pl.ds(first * HD, tiles * HD), :]

    def y_copy(direction, k, p):
        if direction == 0:
            src, dst, dev = (8 - k) % 8, 7 - k, up
        else:
            src, dst, dev = k, k + 1, down
        return remote(w_rows(src, p), w_rows(dst, p), y_send.at[direction, k, p], w_recv.at[dst, p], dev)

    def y_goes(direction, k, p):
        return k < 3 or p // 2 == direction

    def w_wait(slot, p):
        rows = w_rows(slot, p)
        remote(rows, rows, y_send.at[0, 0, 0], w_recv.at[slot, p], up).wait_recv()

    def hz_wait(match, rel, tb, sub):
        tiles = 3 if match == 0 else 2
        rows = hbuf.at[pl.ds((0 if match == 0 else 6) + rel * tiles, tiles), sub, pl.ds(tb * SUB, SUB), :]
        remote(rows, rows, hx_send.at[0, 0, 0], hz_recv.at[rel, tb, sub], right).wait_recv()

    def h_rows(match, tp, sub):
        tiles = pl.ds(0, 6) if match == 0 else pl.ds(6, 4)
        return hbuf.at[tiles, sub, pl.ds(tp * 2 * SUB, 2 * SUB), :]

    def h_wait(match, tp, sub):
        rows = h_rows(match, tp, sub)
        remote(rows, rows, hx_send.at[0, 0, 0], hx_recv.at[match, tp, sub], right).wait_recv()

    def hx_copy(match, tp, sub, direction):
        rows = h_rows(match, tp, sub)
        return remote(
            rows, rows, hx_send.at[direction, tp, sub], hx_recv.at[match, tp, sub],
            right if direction == 0 else left,
        )

    def start_y(k, p):
        for direction in range(2):
            if y_goes(direction, k, p):
                y_copy(direction, k, p).start()

    start_y(0, 0)
    w0_copy(1).start()

    for sub in range(SUBS):
        if sub == LATE:
            w0_copy(2).start()
            w0_copy(3).start()
        for plane in (1, 0):
            for match in range(2):
                cond, first, copy = h0_copy(match, plane, sub)

                @pl.when(cond)
                def _():
                    copy.start()

    if LATE == SUBS:
        w0_copy(2).start()
        w0_copy(3).start()
    for k in range(1, 8):
        s_copy(k).start()

    rel_own = lax.rem(zh + pair, 2)
    for match in range(2):
        tiles, start = (3, 0) if match == 0 else (2, 3)

        @pl.when(is_root & (side == lax.rem(x // 2 + match, 2)))
        def _():
            for sub in range(SUBS):
                for kt in range(tiles):
                    hbuf[rel_own * tiles + (0 if match == 0 else 6) + kt, sub, pl.ds(own_tb * SUB, SUB), :] = hid[
                        start + kt, sub * SUB:(sub + 1) * SUB, :
                    ]

    root_match = x // 2 == side
    left_match = lax.rem(x + 3, 4) // 2 == side

    def for_match(flag, body):
        @pl.when(flag)
        def _():
            body(0)

        @pl.when(jnp.logical_not(flag))
        def _():
            body(1)

    def h_step(sub):
        @pl.when(is_root)
        def _():
            def root(match):
                for tp in range(2):
                    for tb in (2 * tp, 2 * tp + 1):
                        for rel in range(2):
                            @pl.when(jnp.logical_not((rel_own == rel) & (own_tb == tb)))
                            def _():
                                hz_wait(match, rel, tb, sub)

                    hx_copy(match, tp, sub, 0).start()
                    hx_copy(match, tp, sub, 1).start()

            for_match(root_match, root)

        @pl.when(jnp.logical_not(is_root))
        def _():
            def passer(match):
                h_wait(match, 0, sub)
                hx_copy(match, 0, sub, 0).start()
                h_wait(1 - match, 1, sub)
                hx_copy(1 - match, 1, sub, 1).start()

            for_match(left_match, passer)

    def h_last(sub):
        @pl.when(is_root)
        def _():
            def root(match):
                for tp in range(2):
                    h_wait(1 - match, tp, sub)

            for_match(root_match, root)

        @pl.when(jnp.logical_not(is_root))
        def _():
            def passer(match):
                h_wait(match, 1, sub)
                h_wait(1 - match, 0, sub)

            for_match(left_match, passer)

    def w_step(k, p):
        w_wait(8 - k, p)
        if y_goes(0, k, p):
            y_copy(0, k, p).start()
        w_wait(k, p)
        if y_goes(1, k, p):
            y_copy(1, k, p).start()

    def w_first(p):
        w_wait(0, p)
        start_y(0, p)

    w_first(1)

    w_step(1, 0)
    w_step(1, 1)
    h_step(0)
    w_step(2, 0)
    w_step(2, 1)
    h_step(1)
    w_first(2)
    w_first(3)
    h_step(2)
    w_step(3, 0)
    w_step(3, 1)
    w_step(1, 2)
    w_step(1, 3)
    h_step(3)

    for k in range(1, 8):
        tt = lax.rem(t + k, 8)
        remote(ssqb.at[tt], ssqb.at[tt], s_send.at[0], s_recv.at[tt], right).wait_recv()
    total = jnp.sum(ssqb[...], axis=0)
    for s in range(STEPS):
        mean = jnp.sum(jnp.where(eye, total[s:s + 1, :], 0.0), axis=1, keepdims=True) * F32(1.0 / 5120)
        rtok[s * ROWS:(s + 1) * ROWS, :] = jnp.broadcast_to(lax.rsqrt(mean + EPS), (ROWS, HD))

    def p_copy(u, n):
        lanes = pl.ds(0, HD * len(GROUPS[n]))
        return remote(
            psend.at[u, n, :, :, lanes], px.at[u, n, :, :, lanes], p_send.at[u, n], p_recv.at[u, n], other
        )

    def z_copy(u, n):
        lanes = pl.ds(0, HD * len(GROUPS[n]))
        return remote(
            zsend.at[u, n, :, lanes], qz.at[u, n, :, lanes], z_send.at[u, n], z_recv.at[u, n], partner
        )

    def tokens_of(subs):
        return jnp.concatenate(
            [jnp.concatenate([hbuf[kt, sub] for kt in range(2 * KB // HD)], axis=1) for sub in subs], axis=0
        )

    def subs_of(u):
        return range(u * SUBS // 2, (u + 1) * SUBS // 2)

    def split(part, m, z):
        first_core = part[(m * 4 + z * 2) * SUB:(m * 4 + z * 2 + 1) * SUB, :]
        second_core = part[(m * 4 + z * 2 + 1) * SUB:(m * 4 + z * 2 + 2) * SUB, :]
        return jnp.where(c == 0, first_core, second_core), jnp.where(c == 0, second_core, first_core).astype(BF16)

    def multiply(u, n):
        width = HD * len(GROUPS[n])
        weights = jnp.concatenate([wbuf[d] for d in GROUPS[n]], axis=1)
        part = jnp.dot(tokens_of(subs_of(u)), weights, preferred_element_type=F32)
        for m in range(SUBS // 2):
            for z in range(2):
                keep, send = split(part, m, z)
                pkeep[u, n, z, m * SUB:(m + 1) * SUB, 0:width] = keep
                psend[u, n, z, m * SUB:(m + 1) * SUB, 0:width] = send
        p_copy(u, n).start()

    def second(u, n):
        width = HD * len(GROUPS[n])
        p_copy(u, n).wait_recv()
        zkeep[u, n, :, 0:width] = pkeep[u, n, side, :, 0:width] + px[u, n, side, :, 0:width].astype(F32)
        zsend[u, n, :, 0:width] = (
            pkeep[u, n, 1 - side, :, 0:width] + px[u, n, 1 - side, :, 0:width].astype(F32)
        ).astype(BF16)
        z_copy(u, n).start()

    def finish(queries, rows):
        means = [jnp.mean(query * query, axis=1, keepdims=True) for query in queries]
        queries = [query * lax.rsqrt(mean + EPS) for query, mean in zip(queries, means)]
        cosines, sines = tcos[rows, :], tsin[rows, :]
        return [query * cosines + pltpu.roll(query, 64, 1) * sines for query in queries]

    def third(u):
        rows = slice(u * 2 * ROWS, (u + 1) * 2 * ROWS)
        slots, queries = [], []
        for n in range(len(GROUPS)):
            z_copy(u, n).wait_recv()
        factors = rtok[rows, :]
        for n in range(len(GROUPS)):
            for m, d in enumerate(GROUPS[n]):
                lanes = slice(m * HD, (m + 1) * HD)
                slots.append(d)
                queries.append((zkeep[u, n, :, lanes] + qz[u, n, :, lanes].astype(F32)) * factors)
        for d, turned in zip(slots, finish(queries, rows)):
            head = lax.rem(g + d, 8)
            for m in range(2):
                qbuf[pl.ds(head * STEPS + 2 * u + m, ROWS, stride=HEADS * STEPS), :] = turned[m * ROWS:(m + 1) * ROWS, :]

    def p4_copy():
        return remote(psend4, px4, last_sem.at[0], last_sem.at[1], other)

    def z4_copy():
        return remote(zsend4, qz4, last_sem.at[2], last_sem.at[3], partner)

    def multiply4():
        part = jnp.dot(tokens_of(range(SUBS)), wbuf[4], preferred_element_type=F32)
        for sub in range(SUBS):
            rows = slice(sub * SUB, (sub + 1) * SUB)
            for z in range(2):
                pkeep4[z, rows, :], psend4[z, rows, :] = split(part, sub, z)
        p4_copy().start()

    def second4():
        p4_copy().wait_recv()
        zkeep4[...] = pkeep4[side] + px4[side].astype(F32)
        zsend4[...] = (pkeep4[1 - side] + px4[1 - side].astype(F32)).astype(BF16)
        z4_copy().start()

    def third4():
        z4_copy().wait_recv()
        head = lax.rem(g + 4, 8)
        query = (zkeep4[...] + qz4[...].astype(F32)) * rtok[...]
        turned = finish([query], slice(0, TOK))[0]
        for sub in range(STEPS):
            qbuf[pl.ds(head * STEPS + sub, ROWS, stride=HEADS * STEPS), :] = turned[sub * ROWS:(sub + 1) * ROWS, :]

    def early_sent():
        for k in (1, 2, 3):
            w0_copy(k).wait_send()
        for sub in range(SUBS):
            for plane in range(2):
                for match in range(2):
                    cond, first, copy = h0_copy(match, plane, sub)

                    @pl.when(cond)
                    def _():
                        copy.wait_send()

        for k in range(1, 8):
            s_copy(k).wait_send()
        for k in range(3):
            for p in range(4):
                y_copy(0, k, p).wait_send()
                y_copy(1, k, p).wait_send()
        for sub in range(SUBS):
            @pl.when(is_root)
            def _():
                def root(match):
                    for tp in range(2):
                        hx_copy(match, tp, sub, 0).wait_send()
                        hx_copy(match, tp, sub, 1).wait_send()

                for_match(root_match, root)

            @pl.when(jnp.logical_not(is_root))
            def _():
                def passer(match):
                    hx_copy(match, 0, sub, 0).wait_send()
                    hx_copy(1 - match, 1, sub, 1).wait_send()

                for_match(left_match, passer)

    h_last(0)
    w_step(2, 2)
    w_step(2, 3)
    h_last(1)
    multiply(0, 0)
    multiply(0, 1)
    w_step(3, 2)
    w_step(3, 3)
    second(0, 0)
    second(0, 1)
    h_last(2)
    multiply(0, 2)
    h_last(3)
    multiply(1, 0)
    multiply(1, 1)
    multiply(1, 2)
    second(0, 2)
    early_sent()
    for p in range(4):
        w_wait(4, p)
    multiply4()
    second(1, 0)
    second(1, 1)
    second(1, 2)
    second4()
    third(0)
    third(1)
    third4()

    inputs[5].wait()
    key_at = lax.broadcasted_iota(jnp.int32, (CACHE, HD), 0).astype(F32)
    lane_row = lax.broadcasted_iota(jnp.int32, (CACHE, HD), 1) // 32

    def four_rows(i, carry):
        base = pl.multiple_of(i * 128, 128)
        queries = jnp.transpose(qbuf[pl.ds(base, 128), :]).astype(BF16)
        scores = jnp.zeros((CACHE, HD), F32)
        for r in range(4):
            one = jnp.dot(cacheb[i * 4 + r, :, 0:HD], queries, preferred_element_type=F32)
            scores = one if r == 0 else jnp.where(lane_row == r, one, scores)
        scores = jnp.where(key_at <= last[i, 0:1, :], scores, -jnp.inf)
        raised = jnp.exp(scores - jnp.max(scores, axis=0, keepdims=True))
        weights = raised * (1.0 / jnp.sum(raised, axis=0, keepdims=True))
        weights = jnp.transpose(weights).astype(BF16)
        for r in range(4):
            result = jnp.dot(weights[r * 32:(r + 1) * 32, :], cacheb[i * 4 + r, :, HD:], preferred_element_type=F32)
            out[i * 4 + r] = result.astype(BF16)
        return carry

    lax.fori_loop(0, ROWS // 4, four_rows, 0, unroll=6)

    for p in range(4):
        y_copy(p // 2, 3, p).wait_send()
    for u in range(2):
        for n in range(len(GROUPS)):
            p_copy(u, n).wait_send()
            z_copy(u, n).wait_send()
    p4_copy().wait_send()
    z4_copy().wait_send()


def shards(hidden_in, norm_gain, master_query, query_gain, kv_cache, lengths):
    dma = pltpu.SemaphoreType.DMA
    call = pl.pallas_call(
        kernel,
        out_shape=jax.ShapeDtypeStruct((ROWS, HEADS * STEPS, HD), BF16),
        in_specs=[pl.BlockSpec(memory_space=pltpu.HBM)] * 6,
        out_specs=pl.BlockSpec(memory_space=pltpu.VMEM),
        scratch_shapes=[
            pltpu.VMEM((ROWS, STEPS, KB), BF16),
            pltpu.VMEM((KB // HD * TOK, HD), F32),
            pltpu.VMEM((KB // HD, TOK, HD), BF16),
            pltpu.VMEM((KB,), BF16),
            pltpu.VMEM((KB, HD), F32),
            pltpu.VMEM((HD,), F32),
            pltpu.VMEM((ROWS,), jnp.int32),
            pltpu.VMEM((ROWS, CACHE, 2 * HD), BF16),
            pltpu.VMEM((KB, HD), BF16),
            pltpu.VMEM((HEADS, 2 * KB, HD), BF16),
            pltpu.VMEM((2 * KB // HD, SUBS, 4 * SUB, HD), BF16),
            pltpu.VMEM((8, 8, HD), F32),
            pltpu.VMEM((2, len(GROUPS), 2, 2 * ROWS, WIDE), BF16),
            pltpu.VMEM((2, len(GROUPS), 2, 2 * ROWS, WIDE), F32),
            pltpu.VMEM((2, len(GROUPS), 2, 2 * ROWS, WIDE), BF16),
            pltpu.VMEM((2, len(GROUPS), 2 * ROWS, WIDE), BF16),
            pltpu.VMEM((2, len(GROUPS), 2 * ROWS, WIDE), F32),
            pltpu.VMEM((2, len(GROUPS), 2 * ROWS, WIDE), BF16),
            pltpu.VMEM((2, TOK, HD), BF16),
            pltpu.VMEM((2, TOK, HD), F32),
            pltpu.VMEM((2, TOK, HD), BF16),
            pltpu.VMEM((TOK, HD), BF16),
            pltpu.VMEM((TOK, HD), F32),
            pltpu.VMEM((TOK, HD), BF16),
            pltpu.VMEM((ROWS * HEADS * STEPS, HD), F32),
            pltpu.VMEM((TOK, HD), F32),
            pltpu.VMEM((TOK, HD), F32),
            pltpu.VMEM((TOK, HD), F32),
            pltpu.VMEM((ROWS // 4, 8, HD), F32),
            dma((6,)),
            dma((3,)),
            dma((HEADS, 4)),
            dma((2, 4, 4)),
            dma((2, 2, SUBS)),
            dma((2, 2, SUBS)),
            dma((2, 4, SUBS)),
            dma((2, 2, SUBS)),
            dma((7,)),
            dma((8,)),
            dma((2, len(GROUPS))),
            dma((2, len(GROUPS))),
            dma((2, len(GROUPS))),
            dma((2, len(GROUPS))),
            dma((4,)),
        ],
        compiler_params=pltpu.CompilerParams(
            collective_id=0, has_side_effects=True, vmem_limit_bytes=62 << 20
        ),
    )
    result = call(
        hidden_in,
        norm_gain,
        master_query.reshape(KB, HD),
        query_gain,
        lengths,
        kv_cache.reshape(ROWS, CACHE, 2 * HD),
    )
    return result.reshape(ROWS, HEADS, STEPS, HD).transpose(0, 2, 1, 3).reshape(ROWS, STEPS, HEADS * HD)


def solution(mesh):
    in_specs = (
        P(("group", "fsdp"), None, "tp"),
        P("tp"),
        P("fsdp", "tp", "group"),
        P(),
        P(("group", "fsdp"), "tp", None, None),
        P(("group", "fsdp")),
    )
    out_specs = P(("group", "fsdp"), None, "tp")
    return jax.shard_map(shards, mesh=mesh, in_specs=in_specs, out_specs=out_specs, check_vma=False)
```

```python
import functools

import jax
import jax.numpy as jnp
from jax import lax
from jax.experimental import pallas as pl
from jax.experimental.pallas import tpu as pltpu
from jax.sharding import PartitionSpec as P

MESH = pl.DeviceIdType.MESH
HD = 128
BLK = 128
EPS = 1e-06
ROWS = 48
STEPS = 4
TOK = ROWS * STEPS
KB = 640
HEADS = 8
CACHE = 128
SUBS = 4
LATE = 2
SUB = TOK // SUBS
PIECES = ((0, 3), (6, 2), (3, 3), (8, 2))
F32 = jnp.float32
BF16 = jnp.bfloat16

GROUPS = ((0, 7, 1), (6, 2), (5, 3))
WIDE = 3 * HD


def remote(src, dst, send_sem, recv_sem, device):
    return pltpu.make_async_remote_copy(
        src_ref=src,
        dst_ref=dst,
        send_sem=send_sem,
        recv_sem=recv_sem,
        device_id=device,
        device_id_type=MESH,
    )


def kernel(
    hid_in, gain_in, master_in, qgain_in, lens_in, cache, out,
    hidv, hidf, hid, gain, master, qgain, lens, cacheb,
    wown, wbuf, hbuf, ssqb, psend, pkeep, px, zsend, zkeep, qz,
    psend4, pkeep4, px4, zsend4, zkeep4, qz4, qbuf, tcos, tsin, rtok, last,
    in_sem, w0_send, w_recv, y_send, h0_send, hx_send, hz_recv, hx_recv, s_send, s_recv,
    p_send, p_recv, z_send, z_recv, last_sem,
):
    g, f, t = lax.axis_index("group"), lax.axis_index("fsdp"), lax.axis_index("tp")
    zl, c = f // 2, f % 2
    zh, x = t // 4, t % 4
    side, pair = zl % 2, zl // 2
    up, down = (lax.rem(g + 1, 8), f, t), (lax.rem(g + 7, 8), f, t)
    right = (g, f, zh * 4 + lax.rem(x + 1, 4))
    left = (g, f, zh * 4 + lax.rem(x + 3, 4))
    other = (g, zl * 2 + (1 - c), t)
    partner = (g, (pair * 2 + (1 - side)) * 2 + c, t)
    is_root = c == x % 2
    own_tb = side * 2 + c
    inputs = [
        pltpu.make_async_copy(src, dst, in_sem.at[i])
        for i, (src, dst) in enumerate(
            ((master_in, master), (hid_in, hidv), (gain_in, gain), (qgain_in, qgain), (lens_in, lens), (cache, cacheb))
        )
    ]
    for copy in inputs:
        copy.start()

    def z_at(k):
        k_pair, k_side = k // 2, k % 2
        return (g, (lax.rem(pair + k_pair, 2) * 2 + lax.rem(side + k_side, 2)) * 2 + c, t)

    bar = pltpu.get_barrier_semaphore()

    def tell(device):
        pl.semaphore_signal(bar, inc=1, device_id=device, device_id_type=MESH)

    for k in range(1, 4):
        tell(z_at(k))

    for src_zh in range(2):
        for tb in range(4):
            src_f = pair * 4 + tb

            @pl.when(is_root & jnp.logical_not((src_f == f) & (zh == src_zh)))
            def _():
                tell((g, src_f, src_zh * 4 + x))

    for device in (up, down, right, left, other, partner):
        tell(device)
    for k in range(1, 8):
        tell((g, f, lax.rem(t + k, 8)))

    inputs[0].wait()
    for blk in range(KB // BLK):
        piece = master[blk * BLK:(blk + 1) * BLK, :]
        largest = jnp.max(jnp.abs(piece), axis=(0, 1), keepdims=True)
        scale = (largest + EPS) / 127.0
        scale = scale.astype(BF16).astype(F32)
        level = jnp.floor(piece / scale + 0.5)
        wown[blk * BLK:(blk + 1) * BLK, :] = (level * scale).astype(BF16)

    wbuf[0, 0:3 * HD, :] = wown[0:3 * HD, :]

    inputs[1].wait()
    inputs[2].wait()
    eye = lax.broadcasted_iota(jnp.int32, (ROWS, HD), 0) == lax.broadcasted_iota(jnp.int32, (ROWS, HD), 1)
    for kt in range(KB // HD):
        hidf[kt * TOK:(kt + 1) * TOK, :] = hidv[:, :, kt * HD:(kt + 1) * HD].astype(F32).reshape(TOK, HD)
    gains = gain[...].astype(F32).reshape(1, KB)
    ssq_rows = []
    for s in range(STEPS):
        squares = jnp.zeros((ROWS, HD), F32)
        for kt in range(KB // HD):
            piece = hidf[pl.ds(kt * TOK + s, ROWS, stride=STEPS), :]
            squares += piece * piece
            hid[kt, s * ROWS:(s + 1) * ROWS, :] = (piece * gains[:, kt * HD:(kt + 1) * HD]).astype(BF16)
        ssq_rows.append(
            jnp.sum(jnp.where(eye, jnp.sum(squares, axis=1, keepdims=True), 0.0), axis=0, keepdims=True)
        )
    ssqb[t] = jnp.concatenate(ssq_rows + [jnp.zeros((8 - STEPS, HD), F32)], axis=0)

    inputs[3].wait()
    inputs[4].wait()
    lens_row = lens[...].astype(F32).reshape(1, ROWS)
    lens_wide = jnp.concatenate([lens_row, jnp.zeros((1, HD - ROWS), F32)], axis=1)
    column = jnp.sum(jnp.where(eye, lens_wide, 0.0), axis=1, keepdims=True)
    lane = lax.broadcasted_iota(jnp.int32, (1, HD), 1)
    frequency = jnp.exp((lane % 64).astype(F32) * F32(-2.0 / HD * 13.815510557964274))
    sign = jnp.where(lane < 64, -1.0, 1.0).astype(F32)
    gain_row = qgain[...].reshape(1, HD) * F32(HD ** -0.5)
    gain_far = pltpu.roll(jnp.broadcast_to(gain_row, (8, HD)), 64, 1)[0:1, :] * sign
    for s in range(STEPS):
        angle = (column + F32(s - STEPS)) * frequency
        tcos[s * ROWS:(s + 1) * ROWS, :] = jnp.cos(angle) * gain_row
        tsin[s * ROWS:(s + 1) * ROWS, :] = jnp.sin(angle) * gain_far
    row_at = lax.broadcasted_iota(jnp.int32, (ROWS, HD), 0)
    lane_at = lax.broadcasted_iota(jnp.int32, (ROWS, HD), 1)
    for i in range(ROWS // 4):
        chosen = jnp.sum(jnp.where(row_at == 4 * i + lane_at // 32, column, 0.0), axis=0, keepdims=True)
        last[i] = jnp.broadcast_to(chosen + (lane % STEPS - STEPS).astype(F32), (8, HD))

    pl.semaphore_wait(bar, 3 + 6 + 7 + jnp.where(is_root, 3, 4))

    def w0_copy(k):
        first, tiles = PIECES[k]
        start = 0 if tiles == 3 else 3
        return remote(
            wown.at[pl.ds(start * HD, tiles * HD), :], w_rows(0, k), w0_send.at[k - 1], w_recv.at[0, k], z_at(k)
        )

    def h0_copy(match, plane, sub):
        tiles, start = (3, 0) if match == 0 else (2, 3)
        dst_side = lax.rem(x // 2 + match, 2)
        dst_f = (pair * 2 + dst_side) * 2 + x % 2
        rel = lax.rem(zh + pair, 2)
        same = is_root & (side == dst_side) if plane == 0 else jnp.bool_(False)
        first = rel * tiles + (0 if match == 0 else 6)
        return jnp.logical_not(same), first, remote(
            hid.at[pl.ds(start, tiles), pl.ds(sub * SUB, SUB), :],
            hbuf.at[pl.ds(first, tiles), sub, pl.ds(own_tb * SUB, SUB), :],
            h0_send.at[match, plane, sub],
            hz_recv.at[rel, own_tb, sub],
            (g, dst_f, (zh if plane == 0 else 1 - zh) * 4 + x),
        )

    def s_copy(k):
        return remote(ssqb.at[t], ssqb.at[t], s_send.at[k - 1], s_recv.at[t], (g, f, lax.rem(t + k, 8)))

    def w_rows(slot, p):
        first, tiles = PIECES[p]
        return wbuf.at[slot, pl.ds(first * HD, tiles * HD), :]

    def y_copy(direction, k, p):
        if direction == 0:
            src, dst, dev = (8 - k) % 8, 7 - k, up
        else:
            src, dst, dev = k, k + 1, down
        return remote(w_rows(src, p), w_rows(dst, p), y_send.at[direction, k, p], w_recv.at[dst, p], dev)

    def y_goes(direction, k, p):
        return k < 3 or p // 2 == direction

    def w_wait(slot, p):
        rows = w_rows(slot, p)
        remote(rows, rows, y_send.at[0, 0, 0], w_recv.at[slot, p], up).wait_recv()

    def hz_wait(match, rel, tb, sub):
        tiles = 3 if match == 0 else 2
        rows = hbuf.at[pl.ds((0 if match == 0 else 6) + rel * tiles, tiles), sub, pl.ds(tb * SUB, SUB), :]
        remote(rows, rows, hx_send.at[0, 0, 0], hz_recv.at[rel, tb, sub], right).wait_recv()

    def h_rows(match, tp, sub):
        tiles = pl.ds(0, 6) if match == 0 else pl.ds(6, 4)
        return hbuf.at[tiles, sub, pl.ds(tp * 2 * SUB, 2 * SUB), :]

    def h_wait(match, tp, sub):
        rows = h_rows(match, tp, sub)
        remote(rows, rows, hx_send.at[0, 0, 0], hx_recv.at[match, tp, sub], right).wait_recv()

    def hx_copy(match, tp, sub, direction):
        rows = h_rows(match, tp, sub)
        return remote(
            rows, rows, hx_send.at[direction, tp, sub], hx_recv.at[match, tp, sub],
            right if direction == 0 else left,
        )

    def start_y(k, p):
        for direction in range(2):
            if y_goes(direction, k, p):
                y_copy(direction, k, p).start()

    start_y(0, 0)
    w0_copy(1).start()

    for sub in range(SUBS):
        if sub == LATE:
            w0_copy(2).start()
            w0_copy(3).start()
        for plane in (1, 0):
            for match in range(2):
                cond, first, copy = h0_copy(match, plane, sub)

                @pl.when(cond)
                def _():
                    copy.start()

    if LATE == SUBS:
        w0_copy(2).start()
        w0_copy(3).start()
    for k in range(1, 8):
        s_copy(k).start()

    rel_own = lax.rem(zh + pair, 2)
    for match in range(2):
        tiles, start = (3, 0) if match == 0 else (2, 3)

        @pl.when(is_root & (side == lax.rem(x // 2 + match, 2)))
        def _():
            for sub in range(SUBS):
                for kt in range(tiles):
                    hbuf[rel_own * tiles + (0 if match == 0 else 6) + kt, sub, pl.ds(own_tb * SUB, SUB), :] = hid[
                        start + kt, sub * SUB:(sub + 1) * SUB, :
                    ]

    root_match = x // 2 == side
    left_match = lax.rem(x + 3, 4) // 2 == side

    def for_match(flag, body):
        @pl.when(flag)
        def _():
            body(0)

        @pl.when(jnp.logical_not(flag))
        def _():
            body(1)

    def h_step(sub):
        @pl.when(is_root)
        def _():
            def root(match):
                for tp in range(2):
                    for tb in (2 * tp, 2 * tp + 1):
                        for rel in range(2):
                            @pl.when(jnp.logical_not((rel_own == rel) & (own_tb == tb)))
                            def _():
                                hz_wait(match, rel, tb, sub)

                    hx_copy(match, tp, sub, 0).start()
                    hx_copy(match, tp, sub, 1).start()

            for_match(root_match, root)

        @pl.when(jnp.logical_not(is_root))
        def _():
            def passer(match):
                h_wait(match, 0, sub)
                hx_copy(match, 0, sub, 0).start()
                h_wait(1 - match, 1, sub)
                hx_copy(1 - match, 1, sub, 1).start()

            for_match(left_match, passer)

    def h_last(sub):
        @pl.when(is_root)
        def _():
            def root(match):
                for tp in range(2):
                    h_wait(1 - match, tp, sub)

            for_match(root_match, root)

        @pl.when(jnp.logical_not(is_root))
        def _():
            def passer(match):
                h_wait(match, 1, sub)
                h_wait(1 - match, 0, sub)

            for_match(left_match, passer)

    def w_step(k, p):
        w_wait(8 - k, p)
        if y_goes(0, k, p):
            y_copy(0, k, p).start()
        w_wait(k, p)
        if y_goes(1, k, p):
            y_copy(1, k, p).start()

    def w_first(p):
        w_wait(0, p)
        start_y(0, p)

    w_first(1)

    w_step(1, 0)
    w_step(1, 1)
    h_step(0)
    w_step(2, 0)
    w_step(2, 1)
    h_step(1)
    w_first(2)
    w_first(3)
    h_step(2)
    w_step(3, 0)
    w_step(3, 1)
    w_step(1, 2)
    w_step(1, 3)
    h_step(3)

    for k in range(1, 8):
        tt = lax.rem(t + k, 8)
        remote(ssqb.at[tt], ssqb.at[tt], s_send.at[0], s_recv.at[tt], right).wait_recv()
    total = jnp.sum(ssqb[...], axis=0)
    for s in range(STEPS):
        mean = jnp.sum(jnp.where(eye, total[s:s + 1, :], 0.0), axis=1, keepdims=True) * F32(1.0 / 5120)
        rtok[s * ROWS:(s + 1) * ROWS, :] = jnp.broadcast_to(lax.rsqrt(mean + EPS), (ROWS, HD))

    def p_copy(u, n):
        lanes = pl.ds(0, HD * len(GROUPS[n]))
        return remote(
            psend.at[u, n, :, :, lanes], px.at[u, n, :, :, lanes], p_send.at[u, n], p_recv.at[u, n], other
        )

    def z_copy(u, n):
        lanes = pl.ds(0, HD * len(GROUPS[n]))
        return remote(
            zsend.at[u, n, :, lanes], qz.at[u, n, :, lanes], z_send.at[u, n], z_recv.at[u, n], partner
        )

    def tokens_of(subs):
        return jnp.concatenate(
            [jnp.concatenate([hbuf[kt, sub] for kt in range(2 * KB // HD)], axis=1) for sub in subs], axis=0
        )

    def subs_of(u):
        return range(u * SUBS // 2, (u + 1) * SUBS // 2)

    def split(part, m, z):
        first_core = part[(m * 4 + z * 2) * SUB:(m * 4 + z * 2 + 1) * SUB, :]
        second_core = part[(m * 4 + z * 2 + 1) * SUB:(m * 4 + z * 2 + 2) * SUB, :]
        return jnp.where(c == 0, first_core, second_core), jnp.where(c == 0, second_core, first_core).astype(BF16)

    def multiply(u, n):
        width = HD * len(GROUPS[n])
        weights = jnp.concatenate([wbuf[d] for d in GROUPS[n]], axis=1)
        part = jnp.dot(tokens_of(subs_of(u)), weights, preferred_element_type=F32)
        for m in range(SUBS // 2):
            for z in range(2):
                keep, send = split(part, m, z)
                pkeep[u, n, z, m * SUB:(m + 1) * SUB, 0:width] = keep
                psend[u, n, z, m * SUB:(m + 1) * SUB, 0:width] = send
        p_copy(u, n).start()

    def second(u, n):
        width = HD * len(GROUPS[n])
        p_copy(u, n).wait_recv()
        zkeep[u, n, :, 0:width] = pkeep[u, n, side, :, 0:width] + px[u, n, side, :, 0:width].astype(F32)
        zsend[u, n, :, 0:width] = (
            pkeep[u, n, 1 - side, :, 0:width] + px[u, n, 1 - side, :, 0:width].astype(F32)
        ).astype(BF16)
        z_copy(u, n).start()

    def finish(queries, rows):
        means = [jnp.mean(query * query, axis=1, keepdims=True) for query in queries]
        queries = [query * lax.rsqrt(mean + EPS) for query, mean in zip(queries, means)]
        cosines, sines = tcos[rows, :], tsin[rows, :]
        return [query * cosines + pltpu.roll(query, 64, 1) * sines for query in queries]

    def third(u):
        rows = slice(u * 2 * ROWS, (u + 1) * 2 * ROWS)
        slots, queries = [], []
        for n in range(len(GROUPS)):
            z_copy(u, n).wait_recv()
        factors = rtok[rows, :]
        for n in range(len(GROUPS)):
            for m, d in enumerate(GROUPS[n]):
                lanes = slice(m * HD, (m + 1) * HD)
                slots.append(d)
                queries.append((zkeep[u, n, :, lanes] + qz[u, n, :, lanes].astype(F32)) * factors)
        for d, turned in zip(slots, finish(queries, rows)):
            head = lax.rem(g + d, 8)
            for m in range(2):
                qbuf[pl.ds(head * STEPS + 2 * u + m, ROWS, stride=HEADS * STEPS), :] = turned[m * ROWS:(m + 1) * ROWS, :]

    def p4_copy():
        return remote(psend4, px4, last_sem.at[0], last_sem.at[1], other)

    def z4_copy():
        return remote(zsend4, qz4, last_sem.at[2], last_sem.at[3], partner)

    def multiply4():
        part = jnp.dot(tokens_of(range(SUBS)), wbuf[4], preferred_element_type=F32)
        for sub in range(SUBS):
            rows = slice(sub * SUB, (sub + 1) * SUB)
            for z in range(2):
                pkeep4[z, rows, :], psend4[z, rows, :] = split(part, sub, z)
        p4_copy().start()

    def second4():
        p4_copy().wait_recv()
        zkeep4[...] = pkeep4[side] + px4[side].astype(F32)
        zsend4[...] = (pkeep4[1 - side] + px4[1 - side].astype(F32)).astype(BF16)
        z4_copy().start()

    def third4():
        z4_copy().wait_recv()
        head = lax.rem(g + 4, 8)
        query = (zkeep4[...] + qz4[...].astype(F32)) * rtok[...]
        turned = finish([query], slice(0, TOK))[0]
        for sub in range(STEPS):
            qbuf[pl.ds(head * STEPS + sub, ROWS, stride=HEADS * STEPS), :] = turned[sub * ROWS:(sub + 1) * ROWS, :]

    def early_sent():
        for k in (1, 2, 3):
            w0_copy(k).wait_send()
        for sub in range(SUBS):
            for plane in range(2):
                for match in range(2):
                    cond, first, copy = h0_copy(match, plane, sub)

                    @pl.when(cond)
                    def _():
                        copy.wait_send()

        for k in range(1, 8):
            s_copy(k).wait_send()
        for k in range(3):
            for p in range(4):
                y_copy(0, k, p).wait_send()
                y_copy(1, k, p).wait_send()
        for sub in range(SUBS):
            @pl.when(is_root)
            def _():
                def root(match):
                    for tp in range(2):
                        hx_copy(match, tp, sub, 0).wait_send()
                        hx_copy(match, tp, sub, 1).wait_send()

                for_match(root_match, root)

            @pl.when(jnp.logical_not(is_root))
            def _():
                def passer(match):
                    hx_copy(match, 0, sub, 0).wait_send()
                    hx_copy(1 - match, 1, sub, 1).wait_send()

                for_match(left_match, passer)

    h_last(0)
    w_step(2, 2)
    w_step(2, 3)
    h_last(1)
    multiply(0, 0)
    multiply(0, 1)
    w_step(3, 2)
    w_step(3, 3)
    second(0, 0)
    second(0, 1)
    h_last(2)
    multiply(0, 2)
    h_last(3)
    multiply(1, 0)
    multiply(1, 1)
    multiply(1, 2)
    second(0, 2)
    second(1, 0)
    second(1, 1)
    for p in range(4):
        w_wait(4, p)
    multiply4()
    second(1, 2)
    second4()
    third(0)
    third(1)
    early_sent()
    third4()

    inputs[5].wait()
    key_at = lax.broadcasted_iota(jnp.int32, (CACHE, HD), 0).astype(F32)
    lane_row = lax.broadcasted_iota(jnp.int32, (CACHE, HD), 1) // 32

    def four_rows(i, carry):
        base = pl.multiple_of(i * 128, 128)
        queries = jnp.transpose(qbuf[pl.ds(base, 128), :]).astype(BF16)
        scores = jnp.zeros((CACHE, HD), F32)
        for r in range(4):
            one = jnp.dot(cacheb[i * 4 + r, :, 0:HD], queries, preferred_element_type=F32)
            scores = one if r == 0 else jnp.where(lane_row == r, one, scores)
        scores = jnp.where(key_at <= last[i, 0:1, :], scores, -jnp.inf)
        raised = jnp.exp(scores - jnp.max(scores, axis=0, keepdims=True))
        weights = raised * (1.0 / jnp.sum(raised, axis=0, keepdims=True))
        weights = jnp.transpose(weights).astype(BF16)
        for r in range(4):
            result = jnp.dot(weights[r * 32:(r + 1) * 32, :], cacheb[i * 4 + r, :, HD:], preferred_element_type=F32)
            out[i * 4 + r] = result.astype(BF16)
        return carry

    lax.fori_loop(0, ROWS // 4, four_rows, 0, unroll=6)

    for p in range(4):
        y_copy(p // 2, 3, p).wait_send()
    for u in range(2):
        for n in range(len(GROUPS)):
            p_copy(u, n).wait_send()
            z_copy(u, n).wait_send()
    p4_copy().wait_send()
    z4_copy().wait_send()


def shards(hidden_in, norm_gain, master_query, query_gain, kv_cache, lengths):
    dma = pltpu.SemaphoreType.DMA
    call = pl.pallas_call(
        kernel,
        out_shape=jax.ShapeDtypeStruct((ROWS, HEADS * STEPS, HD), BF16),
        in_specs=[pl.BlockSpec(memory_space=pltpu.HBM)] * 6,
        out_specs=pl.BlockSpec(memory_space=pltpu.VMEM),
        scratch_shapes=[
            pltpu.VMEM((ROWS, STEPS, KB), BF16),
            pltpu.VMEM((KB // HD * TOK, HD), F32),
            pltpu.VMEM((KB // HD, TOK, HD), BF16),
            pltpu.VMEM((KB,), BF16),
            pltpu.VMEM((KB, HD), F32),
            pltpu.VMEM((HD,), F32),
            pltpu.VMEM((ROWS,), jnp.int32),
            pltpu.VMEM((ROWS, CACHE, 2 * HD), BF16),
            pltpu.VMEM((KB, HD), BF16),
            pltpu.VMEM((HEADS, 2 * KB, HD), BF16),
            pltpu.VMEM((2 * KB // HD, SUBS, 4 * SUB, HD), BF16),
            pltpu.VMEM((8, 8, HD), F32),
            pltpu.VMEM((2, len(GROUPS), 2, 2 * ROWS, WIDE), BF16),
            pltpu.VMEM((2, len(GROUPS), 2, 2 * ROWS, WIDE), F32),
            pltpu.VMEM((2, len(GROUPS), 2, 2 * ROWS, WIDE), BF16),
            pltpu.VMEM((2, len(GROUPS), 2 * ROWS, WIDE), BF16),
            pltpu.VMEM((2, len(GROUPS), 2 * ROWS, WIDE), F32),
            pltpu.VMEM((2, len(GROUPS), 2 * ROWS, WIDE), BF16),
            pltpu.VMEM((2, TOK, HD), BF16),
            pltpu.VMEM((2, TOK, HD), F32),
            pltpu.VMEM((2, TOK, HD), BF16),
            pltpu.VMEM((TOK, HD), BF16),
            pltpu.VMEM((TOK, HD), F32),
            pltpu.VMEM((TOK, HD), BF16),
            pltpu.VMEM((ROWS * HEADS * STEPS, HD), F32),
            pltpu.VMEM((TOK, HD), F32),
            pltpu.VMEM((TOK, HD), F32),
            pltpu.VMEM((TOK, HD), F32),
            pltpu.VMEM((ROWS // 4, 8, HD), F32),
            dma((6,)),
            dma((3,)),
            dma((HEADS, 4)),
            dma((2, 4, 4)),
            dma((2, 2, SUBS)),
            dma((2, 2, SUBS)),
            dma((2, 4, SUBS)),
            dma((2, 2, SUBS)),
            dma((7,)),
            dma((8,)),
            dma((2, len(GROUPS))),
            dma((2, len(GROUPS))),
            dma((2, len(GROUPS))),
            dma((2, len(GROUPS))),
            dma((4,)),
        ],
        compiler_params=pltpu.CompilerParams(
            collective_id=0, has_side_effects=True, vmem_limit_bytes=62 << 20
        ),
    )
    result = call(
        hidden_in,
        norm_gain,
        master_query.reshape(KB, HD),
        query_gain,
        lengths,
        kv_cache.reshape(ROWS, CACHE, 2 * HD),
    )
    return result.reshape(ROWS, HEADS, STEPS, HD).transpose(0, 2, 1, 3).reshape(ROWS, STEPS, HEADS * HD)


def solution(mesh):
    in_specs = (
        P(("group", "fsdp"), None, "tp"),
        P("tp"),
        P("fsdp", "tp", "group"),
        P(),
        P(("group", "fsdp"), "tp", None, None),
        P(("group", "fsdp")),
    )
    out_specs = P(("group", "fsdp"), None, "tp")
    return jax.shard_map(shards, mesh=mesh, in_specs=in_specs, out_specs=out_specs, check_vma=False)
```
